512 devices in a mesh: replica: 8 (over y), fsdp: 64 (over x, z, core).
Axes of the slice: x: 4, y: 8, z: 8, core: 2. Of those that a mesh axis runs over, the one named last changes fastest.
Arguments:
- grads: bfloat16 [8, 2, 1024, 8192], P('replica', None, 'fsdp'), may hold values from -16 to 16
- errors: float32 [8, 2, 1024, 8192], P('replica', None, 'fsdp'), may hold values from -4 to 4
- basis: float32 [8192, 2, 32], P('fsdp'), may hold values from -6 to 6
Outputs:
- new_errors: float32 [8, 2, 1024, 8192], P('replica', None, 'fsdp')
- left_factor: float32 [2, 1024, 32], P(None, 'fsdp')
- new_basis: float32 [8192, 2, 32], P('fsdp')
The draws below stay inside these ranges and needn't reach their ends.
All inputs are finite; a program needn't handle non-finite values.
Results may differ from the reference program's by a relative error of at most 0.0003.
Values sent between devices are 32-bit elements; how exact they have to be, the bound alone decides.
No kernel may reach another device: no remote copies, remote signals or barrier semaphores. Data moves between devices by JAX's collectives and lax.ppermute only.
A program may use at most 64 MiB of HBM per device.

```python
import jax
import jax.numpy as jnp
from jax import lax

D = 8192
MROWS = 1024
RANK = 32
NMAT = 2
REPLICAS = 8


def strengthened(drawn, rng, source, target, blocks, factor):
    owner, partner = [(jnp.arange(drawn.shape[dim]) // (drawn.shape[dim] // blocks)).reshape([-1 if axis == dim else 1 for axis in range(drawn.ndim)]) for dim in (source, target)]
    chosen = jax.random.permutation(rng, blocks)[partner]
    strong = (owner == chosen) | (owner == (partner + blocks // 2) % blocks)
    return jnp.where(strong, factor * drawn, drawn)


def block_levels(own_key, dims, split, smallest, largest):
    def one(axis_at, shards_of):
        steps = jax.random.uniform(jax.random.fold_in(jax.random.fold_in(own_key, 6), axis_at), (shards_of,), jnp.float32, smallest / len(split), largest / len(split))
        return jnp.repeat(jnp.exp(steps), dims[axis_at] // shards_of).reshape((-1,) + (1,) * (len(dims) - axis_at - 1))

    factor_of = one(*split[0])
    for cut in split[1:]:
        factor_of = factor_of * one(*cut)
    return factor_of


def bell_draw(stream_key, dims, width, most, pieces=(), held_as=jnp.bfloat16):
    values = width * jax.random.normal(stream_key, dims, jnp.float32)
    if pieces:
        values = values * block_levels(stream_key, dims, pieces, -0.22, 0.18)
    return jnp.clip(values, -most, most).astype(held_as)


def gaussian_with(stream_key, shape, deviation, most, split, heavy, dtype=jnp.bfloat16):
    drawn = deviation * jax.random.normal(stream_key, shape, jnp.float32)
    if split:
        drawn = drawn * block_levels(stream_key, shape, split, -0.22, 0.18)
    return jnp.clip(strengthened(drawn, jax.random.fold_in(stream_key, 3), *heavy), -most, most).astype(dtype)


def setup_inputs(seed: int = 0) -> dict:
    keys = jax.random.split(jax.random.key(seed), 4)
    grads = gaussian_with(keys[0], (REPLICAS, NMAT, MROWS, D), 1.0, 16.0, ((0, 8), (2, 64)), (2, 3, 64, 4.0))
    errors = bell_draw(keys[1], (REPLICAS, NMAT, MROWS, D), 0.3, 4.0, ((0, 8), (2, 64)), jnp.float32)
    basis = bell_draw(keys[2], (D, NMAT, RANK), 1.0, 6.0, ((0, 64),), jnp.float32)
    return {"grads": grads, "errors": errors, "basis": basis}


def orthonormal(factor):
    gram = jnp.einsum('mrk,mrl->mkl', factor, factor, precision=lax.Precision.HIGHEST)
    chol = jnp.linalg.cholesky(gram)

    def solve_one(lower, block):
        return jax.scipy.linalg.solve_triangular(lower, block.T, lower=True).T
    return jax.vmap(solve_one)(chol, factor)

def reference(grads, errors, basis):
    highest = lax.Precision.HIGHEST
    merged = grads.astype(jnp.float32) + errors
    factor = jnp.einsum('amrd,dmk->mrk', merged, basis, precision=highest) / REPLICAS
    left_factor = orthonormal(factor)
    new_basis = jnp.einsum('amrd,mrk->dmk', merged, left_factor, precision=highest) / REPLICAS
    approx = jnp.einsum('mrk,dmk->mrd', left_factor, new_basis, precision=highest)
    new_errors = merged - approx[None]
    return (new_errors, left_factor, new_basis)
```

```python
import jax
import jax.numpy as jnp
from jax import lax
from jax.experimental import pallas as pl
from jax.experimental.pallas import tpu as pltpu
from jax.sharding import Mesh, PartitionSpec as P

NX, NZ, NC = 4, 8, 2
LANES = 128
HIGHEST = lax.Precision.HIGHEST
F32 = jnp.float32
VMEM = pl.BlockSpec(memory_space=pltpu.VMEM)


def cost(flops, moved):
    return pl.CostEstimate(flops=flops, bytes_accessed=moved, transcendentals=0)


def dot(a, b, dims):
    return lax.dot_general(a, b, (dims, ((), ())), precision=HIGHEST, preferred_element_type=F32)


def merge_kernel(grads, errors, out):
    for m in range(2):
        merged = grads[0, m].astype(F32) + errors[0, m]
        for block in range(16):
            out[block, 0, m] = merged[:, block * LANES : (block + 1) * LANES]


def merge(grads, errors):
    _, mats, rows, width = grads.shape
    part = width // NX
    return pl.pallas_call(
        merge_kernel,
        grid=(NX,),
        in_specs=[pl.BlockSpec((1, mats, rows, part), lambda i: (0, 0, 0, i))] * 2,
        out_specs=pl.BlockSpec((16, 1, mats, rows, LANES), lambda i: (0, i, 0, 0, 0)),
        out_shape=jax.ShapeDtypeStruct((16, NX, mats, rows, LANES), F32),
        cost_estimate=cost(2**19, 5 * 2**19),
        name="merge",
    )(grads, errors)


def factor_kernel(recv, b0, b1, b2, b3, mean_out, send):
    x = lax.axis_index("x")
    packed = jnp.stack([b0[...], b1[...], b2[...], b3[...]])
    columns, weights = [], []
    for part in range(NX):
        blocks = []
        for m in range(2):
            for c in range(NC):
                total = recv[c, part, m]
                for a in range(1, 8):
                    total = total + recv[2 * a + c, part, m]
                blocks.append(total)
        columns.append(jnp.concatenate(blocks, axis=0) * 0.125)
        back = lax.rem(x - part + NX, NX)
        chosen = packed[0]
        for k in range(1, NX):
            chosen = jnp.where(back == k, packed[k], chosen)
        weights.append(chosen[:, :64])
        weights.append(chosen[:, 64:])
    mean = jnp.concatenate(columns, axis=1)
    mean_out[...] = mean
    partial = dot(mean, jnp.concatenate(weights, axis=0), ((1,), (0,)))
    piece = jnp.concatenate(
        [
            partial[16 * (2 * m + c) : 16 * (2 * m + c + 1), 32 * m : 32 * (m + 1)]
            for m in range(2)
            for c in range(NC)
        ],
        axis=1,
    )
    for i in range(16):
        send[i] = piece


def factor_part(recv, shards):
    return pl.pallas_call(
        factor_kernel,
        in_specs=[VMEM] * 5,
        out_specs=[VMEM] * 2,
        out_shape=[
            jax.ShapeDtypeStruct((64, 512), F32),
            jax.ShapeDtypeStruct((16, 16, LANES), F32),
        ],
        cost_estimate=cost(2**22, 2**20 + 2**19),
        name="factor_part",
    )(recv, *shards)


def term_kernel(recv, mean, send):
    factor = recv[0]
    for i in range(1, 16):
        factor = factor + recv[i]
    blank = jnp.zeros((16, 32), F32)
    rows = []
    for m in range(2):
        for c in range(NC):
            piece = factor[:, 32 * (2 * m + c) : 32 * (2 * m + c + 1)]
            rows.append(jnp.concatenate([piece, blank] if m == 0 else [blank, piece], axis=1))
    blocked = jnp.concatenate(rows, axis=0)
    term = dot(mean[...], blocked, ((0,), (0,)))
    for g in range(NX * NZ):
        low = term[16 * g : 16 * g + 8]
        high = term[16 * g + 8 : 16 * g + 16]
        send[g, 0:8] = jnp.concatenate([low, high], axis=1)
        send[g, 8:24] = factor


def term_part(recv, mean):
    return pl.pallas_call(
        term_kernel,
        in_specs=[VMEM] * 2,
        out_specs=VMEM,
        out_shape=jax.ShapeDtypeStruct((NX * NZ, 24, LANES), F32),
        cost_estimate=cost(2**23, 2**20),
        name="term_part",
    )(recv, mean)


def spread_kernel(recv, send):
    total = recv[0]
    for g in range(1, NX * NZ):
        total = total + recv[g]
    for i in range(8 * NZ):
        send[i] = total


def spread(recv):
    return pl.pallas_call(
        spread_kernel,
        grid=(1,),
        in_specs=[pl.BlockSpec((NX * NZ, 8, LANES), lambda i: (0, 0, 0))],
        out_specs=pl.BlockSpec((8 * NZ, 8, LANES), lambda i: (0, 0, 0)),
        out_shape=jax.ShapeDtypeStruct((8 * NZ, 8, LANES), F32),
        cost_estimate=cost(2**15, 2**19),
        name="spread",
    )(recv)


def inverse_factors(gram):
    row = lax.broadcasted_iota(jnp.int32, (32, 64), 0)
    lane = lax.broadcasted_iota(jnp.int32, (32, 64), 1)
    left = lane < 32
    unit = jnp.where((lane == row) | (lane == row + 32), 1.0, 0.0).astype(F32)
    scale = jnp.zeros((32, 64), F32)
    for j in range(32):
        column = jnp.where(left, gram[:, j : j + 1], gram[:, 32 + j : 33 + j])
        pivot = column[j : j + 1]
        scale = jnp.where(row == j, pivot, scale)
        share = jnp.where(row > j, column / pivot, 0.0)
        gram = gram - share * gram[j : j + 1]
        unit = unit - share * unit[j : j + 1]
    return unit / jnp.sqrt(scale)


def solve_kernel(recv, solve_out, rows_out, left_out):
    x, z, c = lax.axis_index("x"), lax.axis_index("z"), lax.axis_index("c")
    whole = recv[:, 8:24, :].reshape(NX * NZ * 16, LANES)
    square = dot(whole, whole, ((0,), (0,)))
    grams = []
    for m in range(2):
        a, b = 64 * m, 64 * m + 32
        grams.append(square[a : a + 32, a : a + 32] + square[b : b + 32, b : b + 32])
    inverse = inverse_factors(jnp.concatenate(grams, axis=1))
    blank = jnp.zeros((32, 32), F32)
    parts = [inverse[:, :32], inverse[:, 32:]]
    solve_out[...] = jnp.concatenate(
        [jnp.concatenate([parts[0], blank], axis=1), jnp.concatenate([blank, parts[1]], axis=1)],
        axis=0,
    )
    wide = jnp.concatenate(
        [
            jnp.concatenate([parts[i // 2] if i == j else blank for j in range(4)], axis=1)
            for i in range(4)
        ],
        axis=0,
    )
    mine = jnp.concatenate([recv[part * NZ + z, 8:24, :] for part in range(NX)], axis=0)
    rows = dot(mine, wide, ((1,), (1,)))
    rows_out[...] = rows
    own = rows[0:16]
    for part in range(1, NX):
        own = jnp.where(x == part, rows[16 * part : 16 * part + 16], own)
    for m in range(2):
        left_out[m] = jnp.where(c == 0, own[:, 64 * m : 64 * m + 32], own[:, 64 * m + 32 : 64 * m + 64])


def solve(recv):
    return pl.pallas_call(
        solve_kernel,
        in_specs=[VMEM],
        out_specs=[VMEM] * 3,
        out_shape=[
            jax.ShapeDtypeStruct((64, 64), F32),
            jax.ShapeDtypeStruct((64, LANES), F32),
            jax.ShapeDtypeStruct((2, 16, 32), F32),
        ],
        cost_estimate=cost(2**24, 2**19),
        name="solve",
    )(recv)


def approx_kernel(recv, solver, rows, send, basis_out):
    z = lax.axis_index("z")
    packed = recv[...]
    term = jnp.concatenate([packed[:, :, :64], packed[:, :, 64:]], axis=1).reshape(1024, 64)
    turned = dot(solver[...], term, ((1,), (1,)))
    own = recv[pl.ds(z * NZ, NZ)]
    own = jnp.concatenate([own[:, :, :64], own[:, :, 64:]], axis=1).reshape(LANES, 64)
    basis = dot(own, solver[...], ((1,), (1,)))
    for m in range(2):
        basis_out[:, m, :] = basis[:, 32 * m : 32 * (m + 1)]
        blocks = []
        for part in range(NX):
            for c in range(NC):
                at = 32 * (2 * m + c)
                blocks.append(rows[16 * part : 16 * part + 16, at : at + 32])
        result = dot(jnp.concatenate(blocks, axis=0), turned[32 * m : 32 * (m + 1)], ((1,), (0,)))
        for i in range(NX * NC):
            send[i, m] = result[16 * i : 16 * i + 16]


def approx_part(recv, solver, rows):
    return pl.pallas_call(
        approx_kernel,
        in_specs=[VMEM] * 3,
        out_specs=[VMEM] * 2,
        out_shape=[
            jax.ShapeDtypeStruct((NX * NC, 2, 16, 1024), F32),
            jax.ShapeDtypeStruct((LANES, 2, 32), F32),
        ],
        cost_estimate=cost(2**26, 2**20),
        name="approx_part",
    )(recv, solver, rows)


def subtract_kernel(grads, errors, recv, out):
    for m in range(2):
        merged = grads[0, m].astype(F32) + errors[0, m]
        for a in range(8):
            for c in range(NC):
                at = slice((2 * a + c) * LANES, (2 * a + c + 1) * LANES)
                out[0, m, :, at] = merged[:, at] - recv[c, m, :, a * LANES : (a + 1) * LANES]


def subtract(grads, errors, recv):
    _, mats, rows, width = grads.shape
    part = width // NX
    spec = pl.BlockSpec((1, mats, rows, part), lambda i: (0, 0, 0, i))
    return pl.pallas_call(
        subtract_kernel,
        grid=(NX,),
        in_specs=[spec, spec, pl.BlockSpec((NC, mats, rows, 1024), lambda i: (i, 0, 0, 0))],
        out_specs=spec,
        out_shape=jax.ShapeDtypeStruct(grads.shape, F32),
        cost_estimate=cost(2**19, 7 * 2**19),
        name="subtract",
    )(grads, errors, recv)


def shards(grads, errors, basis):
    send = merge(grads, errors)
    flat = basis.reshape(LANES, 64)
    held = jnp.concatenate([flat[:64], flat[64:]], axis=1)
    held, send = lax.optimization_barrier((held, send))
    recv = lax.all_to_all(send, ("y", "c"), 0, 0)
    held = lax.ppermute(held, ("y", "z"), [(y * NZ + z, z * NZ + y) for y in range(8) for z in range(NZ)])
    parts = [held] + [
        lax.ppermute(held, "x", [(i, (i + k) % NX) for i in range(NX)]) for k in range(1, NX)
    ]
    mean, send = factor_part(recv, parts)
    recv = lax.all_to_all(send, ("y", "c"), 0, 0)
    send = term_part(recv, mean)
    recv = lax.all_to_all(send, ("x", "z"), 0, 0)
    gathered = lax.all_to_all(spread(recv), ("y", "z"), 0, 0)
    solver, rows, left_factor = solve(recv)
    send, new_basis = approx_part(gathered, solver, rows)
    recv = lax.all_to_all(send, ("x", "c"), 0, 0)
    return (subtract(grads, errors, recv), left_factor, new_basis)


def solution(mesh):
    fine = Mesh(mesh.devices.reshape(8, NX, NZ, NC), ("y", "x", "z", "c"))
    fsdp = ("x", "z", "c")
    in_specs = (P("y", None, fsdp, None), P("y", None, fsdp, None), P(fsdp, None, None))
    out_specs = (P("y", None, fsdp, None), P(None, fsdp, None), P(fsdp, None, None))
    return jax.shard_map(shards, mesh=fine, in_specs=in_specs, out_specs=out_specs, check_vma=False)
```

```python
import jax
import jax.numpy as jnp
from jax import lax
from jax.experimental import pallas as pl
from jax.experimental.pallas import tpu as pltpu
from jax.sharding import Mesh, PartitionSpec as P

NX, NZ, NC = 4, 8, 2
LANES = 128
HIGHEST = lax.Precision.HIGHEST
F32 = jnp.float32
VMEM = pl.BlockSpec(memory_space=pltpu.VMEM)
HBM = pl.BlockSpec(memory_space=pltpu.HBM)
PARAMS = pltpu.CompilerParams(vmem_limit_bytes=16 * 2**20)


def cost(flops, moved):
    return pl.CostEstimate(flops=flops, bytes_accessed=moved, transcendentals=0)


def dot(a, b, dims):
    return lax.dot_general(a, b, (dims, ((), ())), precision=HIGHEST, preferred_element_type=F32)


def chunk(x):
    return pl.ds(x * 16 * LANES, 16 * LANES)


def merge_kernel(grads, errors, out, grads_in, errors_in, sems):
    copies = []
    for x in range(NX):
        for k, (source, target) in enumerate(((grads, grads_in), (errors, errors_in))):
            copy = pltpu.make_async_copy(
                source.at[0, :, :, chunk(x)], target.at[:, :, chunk(x)], sems.at[k, x]
            )
            copy.start()
            copies.append(copy)
    for x in range(NX):
        copies[2 * x].wait()
        copies[2 * x + 1].wait()
        for m in range(2):
            for block in range(16):
                at = pl.ds((x * 16 + block) * LANES, LANES)
                out[block, x, m] = grads_in[m, :, at].astype(F32) + errors_in[m, :, at]


def merge(grads, errors):
    _, mats, rows, width = grads.shape
    return pl.pallas_call(
        merge_kernel,
        in_specs=[HBM] * 2,
        out_specs=VMEM,
        out_shape=jax.ShapeDtypeStruct((16, NX, mats, rows, LANES), F32),
        scratch_shapes=[
            pltpu.VMEM((mats, rows, width), grads.dtype),
            pltpu.VMEM((mats, rows, width), errors.dtype),
            pltpu.SemaphoreType.DMA((2, NX)),
        ],
        compiler_params=PARAMS,
        cost_estimate=cost(2**19, 5 * 2**19),
        name="merge",
    )(grads, errors)


def factor_kernel(recv, b0, b1, b2, b3, mean_out, send):
    x = lax.axis_index("x")
    packed = jnp.stack([b0[...], b1[...], b2[...], b3[...]])
    columns, weights = [], []
    for part in range(NX):
        blocks = []
        for m in range(2):
            for c in range(NC):
                total = recv[c, part, m]
                for a in range(1, 8):
                    total = total + recv[2 * a + c, part, m]
                blocks.append(total)
        columns.append(jnp.concatenate(blocks, axis=0) * 0.125)
        back = lax.rem(x - part + NX, NX)
        chosen = packed[0]
        for k in range(1, NX):
            chosen = jnp.where(back == k, packed[k], chosen)
        weights.append(chosen)
    mean = jnp.concatenate(columns, axis=1)
    mean_out[...] = mean
    partial = dot(mean, jnp.concatenate(weights, axis=1), ((1,), (1,)))
    piece = jnp.concatenate(
        [
            partial[16 * (2 * m + c) : 16 * (2 * m + c + 1), 32 * m : 32 * (m + 1)]
            for m in range(2)
            for c in range(NC)
        ],
        axis=1,
    )
    for i in range(16):
        send[i] = piece


def factor_part(recv, shards):
    return pl.pallas_call(
        factor_kernel,
        in_specs=[VMEM] * 5,
        out_specs=[VMEM] * 2,
        out_shape=[
            jax.ShapeDtypeStruct((64, 512), F32),
            jax.ShapeDtypeStruct((16, 16, LANES), F32),
        ],
        compiler_params=PARAMS,
        cost_estimate=cost(2**22, 2**20 + 2**19),
        name="factor_part",
    )(recv, *shards)


def term_kernel(recv, mean, send):
    factor = recv[0]
    for i in range(1, 16):
        factor = factor + recv[i]
    blank = jnp.zeros((16, 32), F32)
    rows = []
    for m in range(2):
        for c in range(NC):
            piece = factor[:, 32 * (2 * m + c) : 32 * (2 * m + c + 1)]
            rows.append(jnp.concatenate([piece, blank] if m == 0 else [blank, piece], axis=1))
    blocked = jnp.concatenate(rows, axis=0)
    term = dot(blocked, mean[...], ((0,), (0,)))
    for x in range(NX):
        for z in range(NZ):
            send[x * NZ + z, 0:8] = term[8 * z : 8 * z + 8, x * LANES : (x + 1) * LANES]
            send[x * NZ + z, 8:24] = factor


def term_part(recv, mean):
    return pl.pallas_call(
        term_kernel,
        in_specs=[VMEM] * 2,
        out_specs=VMEM,
        out_shape=jax.ShapeDtypeStruct((NX * NZ, 24, LANES), F32),
        compiler_params=PARAMS,
        cost_estimate=cost(2**23, 2**20),
        name="term_part",
    )(recv, mean)


def spread_kernel(recv, send):
    total = recv[0, 0:8]
    for g in range(1, NX * NZ):
        total = total + recv[g, 0:8]
    for i in range(8 * NZ):
        send[i] = total


def spread(recv):
    return pl.pallas_call(
        spread_kernel,
        in_specs=[VMEM],
        out_specs=VMEM,
        out_shape=jax.ShapeDtypeStruct((8 * NZ, 8, LANES), F32),
        compiler_params=PARAMS,
        cost_estimate=cost(2**15, 2**19),
        name="spread",
    )(recv)


def inverse_factors(gram):
    row = lax.broadcasted_iota(jnp.int32, (32, 64), 0)
    lane = lax.broadcasted_iota(jnp.int32, (32, 64), 1)
    left = lane < 32
    unit = jnp.where((lane == row) | (lane == row + 32), 1.0, 0.0).astype(F32)
    scale = jnp.zeros((32, 64), F32)
    for j in range(32):
        column = jnp.where(left, gram[:, j : j + 1], gram[:, 32 + j : 33 + j])
        pivot = column[j : j + 1]
        scale = jnp.where(row == j, pivot, scale)
        share = jnp.where(row > j, column / pivot, 0.0)
        gram = gram - share * gram[j : j + 1]
        unit = unit - share * unit[j : j + 1]
    return unit / jnp.sqrt(scale)


def solve_kernel(recv, solve_out, rows_out, left_out):
    x, z, c = lax.axis_index("x"), lax.axis_index("z"), lax.axis_index("c")
    whole = recv[:, 8:24, :].reshape(NX * NZ * 16, LANES)
    square = dot(whole, whole, ((0,), (0,)))
    grams = []
    for m in range(2):
        a, b = 64 * m, 64 * m + 32
        grams.append(square[a : a + 32, a : a + 32] + square[b : b + 32, b : b + 32])
    inverse = inverse_factors(jnp.concatenate(grams, axis=1))
    blank = jnp.zeros((32, 32), F32)
    parts = [inverse[:, :32], inverse[:, 32:]]
    solve_out[...] = jnp.concatenate(
        [jnp.concatenate([parts[0], blank], axis=1), jnp.concatenate([blank, parts[1]], axis=1)],
        axis=0,
    )
    wide = jnp.concatenate(
        [
            jnp.concatenate([parts[i // 2] if i == j else blank for j in range(4)], axis=1)
            for i in range(4)
        ],
        axis=0,
    )
    mine = jnp.concatenate([recv[part * NZ + z, 8:24, :] for part in range(NX)], axis=0)
    rows = dot(mine, wide, ((1,), (1,)))
    rows_out[...] = rows
    own = rows[0:16]
    for part in range(1, NX):
        own = jnp.where(x == part, rows[16 * part : 16 * part + 16], own)
    for m in range(2):
        left_out[m] = jnp.where(c == 0, own[:, 64 * m : 64 * m + 32], own[:, 64 * m + 32 : 64 * m + 64])


def solve(recv):
    return pl.pallas_call(
        solve_kernel,
        in_specs=[VMEM],
        out_specs=[VMEM] * 3,
        out_shape=[
            jax.ShapeDtypeStruct((64, 64), F32),
            jax.ShapeDtypeStruct((64, LANES), F32),
            jax.ShapeDtypeStruct((2, 16, 32), F32),
        ],
        compiler_params=PARAMS,
        cost_estimate=cost(2**24, 2**19),
        name="solve",
    )(recv)


def approx_kernel(recv, solver, rows, send, basis_out):
    z = lax.axis_index("z")
    term = jnp.concatenate(
        [recv[a * NZ : (a + 1) * NZ].reshape(64, LANES) for a in range(8)], axis=1
    )
    turned = dot(solver[...], term, ((1,), (0,)))
    own = turned[:, :LANES]
    for a in range(1, 8):
        own = jnp.where(z == a, turned[:, a * LANES : (a + 1) * LANES], own)
    basis_out[...] = own
    for m in range(2):
        blocks = []
        for part in range(NX):
            for c in range(NC):
                at = 32 * (2 * m + c)
                blocks.append(rows[16 * part : 16 * part + 16, at : at + 32])
        result = dot(jnp.concatenate(blocks, axis=0), turned[32 * m : 32 * (m + 1)], ((1,), (0,)))
        for i in range(NX * NC):
            send[i, m] = result[16 * i : 16 * i + 16]


def approx_part(recv, solver, rows):
    return pl.pallas_call(
        approx_kernel,
        in_specs=[VMEM] * 3,
        out_specs=[VMEM] * 2,
        out_shape=[
            jax.ShapeDtypeStruct((NX * NC, 2, 16, 1024), F32),
            jax.ShapeDtypeStruct((64, LANES), F32),
        ],
        compiler_params=PARAMS,
        cost_estimate=cost(2**26, 2**20),
        name="approx_part",
    )(recv, solver, rows)


def subtract_kernel(merged, recv, out, result, sems):
    copies = []
    for x in range(NX):
        for m in range(2):
            for a in range(8):
                for c in range(NC):
                    at = pl.ds((x * 16 + 2 * a + c) * LANES, LANES)
                    approx = recv[NC * x + c, m, :, a * LANES : (a + 1) * LANES]
                    result[m, :, at] = merged[2 * a + c, x, m] - approx
        copy = pltpu.make_async_copy(
            result.at[:, :, chunk(x)], out.at[0, :, :, chunk(x)], sems.at[x]
        )
        copy.start()
        copies.append(copy)
    for copy in copies:
        copy.wait()


def subtract(merged, recv):
    _, _, mats, rows, _ = merged.shape
    width = NX * 16 * LANES
    return pl.pallas_call(
        subtract_kernel,
        in_specs=[VMEM] * 2,
        out_specs=HBM,
        out_shape=jax.ShapeDtypeStruct((1, mats, rows, width), F32),
        scratch_shapes=[pltpu.VMEM((mats, rows, width), F32), pltpu.SemaphoreType.DMA((NX,))],
        compiler_params=PARAMS,
        cost_estimate=cost(2**19, 7 * 2**19),
        name="subtract",
    )(merged, recv)


def shards(grads, errors, basis):
    held = basis.transpose(1, 2, 0).reshape(64, LANES)
    held = lax.ppermute(held, ("y", "z"), [(y * NZ + z, z * NZ + y) for y in range(8) for z in range(NZ)])
    merged = merge(grads, errors)
    recv = lax.all_to_all(merged, ("y", "c"), 0, 0)
    parts = [held] + [
        lax.ppermute(held, "x", [(i, (i + k) % NX) for i in range(NX)]) for k in range(1, NX)
    ]
    mean, send = factor_part(recv, parts)
    recv = lax.all_to_all(send, ("y", "c"), 0, 0)
    send = term_part(recv, mean)
    recv = lax.all_to_all(send, ("x", "z"), 0, 0)
    gathered = lax.all_to_all(spread(recv), ("y", "z"), 0, 0)
    solver, rows, left_factor = solve(recv)
    send, new_basis = approx_part(gathered, solver, rows)
    recv = lax.all_to_all(send, ("x", "c"), 0, 0)
    new_basis = new_basis.reshape(2, 32, LANES).transpose(2, 0, 1)
    return (subtract(merged, recv), left_factor, new_basis)


def solution(mesh):
    fine = Mesh(mesh.devices.reshape(8, NX, NZ, NC), ("y", "x", "z", "c"))
    fsdp = ("x", "z", "c")
    in_specs = (P("y", None, fsdp, None), P("y", None, fsdp, None), P(fsdp, None, None))
    out_specs = (P("y", None, fsdp, None), P(None, fsdp, None), P(fsdp, None, None))
    return jax.shard_map(shards, mesh=fine, in_specs=in_specs, out_specs=out_specs, check_vma=False)
```

```python
import jax
import jax.numpy as jnp
from jax import lax
from jax.experimental import pallas as pl
from jax.experimental.pallas import tpu as pltpu
from jax.sharding import Mesh, PartitionSpec as P

NX, NZ, NC = 4, 8, 2
LANES = 128
HIGHEST = lax.Precision.HIGHEST
F32 = jnp.float32
VMEM = pl.BlockSpec(memory_space=pltpu.VMEM)
HBM = pl.BlockSpec(memory_space=pltpu.HBM)
PARAMS = pltpu.CompilerParams(vmem_limit_bytes=16 * 2**20)


def cost(flops, moved):
    return pl.CostEstimate(flops=flops, bytes_accessed=moved, transcendentals=0)


def dot(a, b, dims):
    return lax.dot_general(a, b, (dims, ((), ())), precision=HIGHEST, preferred_element_type=F32)


def chunk(x):
    return pl.ds(x * 16 * LANES, 16 * LANES)


def merge_kernel(grads, errors, out, grads_in, errors_in, sems):
    copies = []
    for x in range(NX):
        for k, (source, target) in enumerate(((grads, grads_in), (errors, errors_in))):
            copy = pltpu.make_async_copy(
                source.at[0, :, :, chunk(x)], target.at[:, :, chunk(x)], sems.at[k, x]
            )
            copy.start()
            copies.append(copy)
    for x in range(NX):
        copies[2 * x].wait()
        copies[2 * x + 1].wait()
        for m in range(2):
            for block in range(16):
                at = pl.ds((x * 16 + block) * LANES, LANES)
                out[block, x, m] = grads_in[m, :, at].astype(F32) + errors_in[m, :, at]


def merge(grads, errors):
    _, mats, rows, width = grads.shape
    return pl.pallas_call(
        merge_kernel,
        in_specs=[HBM] * 2,
        out_specs=VMEM,
        out_shape=jax.ShapeDtypeStruct((16, NX, mats, rows, LANES), F32),
        scratch_shapes=[
            pltpu.VMEM((mats, rows, width), grads.dtype),
            pltpu.VMEM((mats, rows, width), errors.dtype),
            pltpu.SemaphoreType.DMA((2, NX)),
        ],
        cost_estimate=cost(2**19, 5 * 2**19),
        name="merge",
    )(grads, errors)


def relay_kernel(block, out):
    out[...] = block[...]


def relay(block):
    return pl.pallas_call(
        relay_kernel,
        in_specs=[VMEM],
        out_specs=VMEM,
        out_shape=jax.ShapeDtypeStruct(block.shape, F32),
        compiler_params=PARAMS,
        cost_estimate=cost(2**35, 2**16),
        name="relay",
    )(block)


def arrange_kernel(b0, b1, b2, b3, out):
    x = lax.axis_index("x")
    for part in range(NX):
        back = lax.rem(x - part + NX, NX)
        chosen = b0[...]
        for k, block in ((1, b1), (2, b2), (3, b3)):
            chosen = jnp.where(back == k, block[...], chosen)
        out[:, part * LANES : (part + 1) * LANES] = chosen


def arrange(shards):
    return pl.pallas_call(
        arrange_kernel,
        in_specs=[VMEM] * 4,
        out_specs=VMEM,
        out_shape=jax.ShapeDtypeStruct((64, NX * LANES), F32),
        compiler_params=PARAMS,
        cost_estimate=cost(2**20, 2**18),
        name="arrange",
    )(*shards)


def factor_kernel(recv, weights, mean_out, send):
    columns = []
    for part in range(NX):
        blocks = []
        for m in range(2):
            for c in range(NC):
                total = recv[c, part, m]
                for a in range(1, 8):
                    total = total + recv[2 * a + c, part, m]
                blocks.append(total)
        columns.append(jnp.concatenate(blocks, axis=0) * 0.125)
    mean = jnp.concatenate(columns, axis=1)
    mean_out[...] = mean
    partial = dot(mean, weights[...], ((1,), (1,)))
    piece = jnp.concatenate(
        [
            partial[16 * (2 * m + c) : 16 * (2 * m + c + 1), 32 * m : 32 * (m + 1)]
            for m in range(2)
            for c in range(NC)
        ],
        axis=1,
    )
    for i in range(16):
        send[i] = piece


def factor_part(recv, weights):
    return pl.pallas_call(
        factor_kernel,
        in_specs=[VMEM] * 2,
        out_specs=[VMEM] * 2,
        out_shape=[
            jax.ShapeDtypeStruct((64, 512), F32),
            jax.ShapeDtypeStruct((16, 16, LANES), F32),
        ],
        compiler_params=PARAMS,
        cost_estimate=cost(2**22, 2**20 + 2**19),
        name="factor_part",
    )(recv, weights)


def term_kernel(recv, mean, send):
    factor = recv[0]
    for i in range(1, 16):
        factor = factor + recv[i]
    blank = jnp.zeros((16, 32), F32)
    rows = []
    for m in range(2):
        for c in range(NC):
            piece = factor[:, 32 * (2 * m + c) : 32 * (2 * m + c + 1)]
            rows.append(jnp.concatenate([piece, blank] if m == 0 else [blank, piece], axis=1))
    blocked = jnp.concatenate(rows, axis=0)
    term = dot(blocked, mean[...], ((0,), (0,)))
    for x in range(NX):
        for z in range(NZ):
            send[x * NZ + z, 0:8] = term[8 * z : 8 * z + 8, x * LANES : (x + 1) * LANES]
            send[x * NZ + z, 8:24] = factor


def term_part(recv, mean):
    return pl.pallas_call(
        term_kernel,
        in_specs=[VMEM] * 2,
        out_specs=VMEM,
        out_shape=jax.ShapeDtypeStruct((NX * NZ, 24, LANES), F32),
        compiler_params=PARAMS,
        cost_estimate=cost(2**23, 2**20),
        name="term_part",
    )(recv, mean)


def spread_kernel(recv, send):
    total = recv[0, 0:8]
    for g in range(1, NX * NZ):
        total = total + recv[g, 0:8]
    for i in range(8 * NZ):
        send[i] = total


def spread(recv):
    return pl.pallas_call(
        spread_kernel,
        in_specs=[VMEM],
        out_specs=VMEM,
        out_shape=jax.ShapeDtypeStruct((8 * NZ, 8, LANES), F32),
        compiler_params=PARAMS,
        cost_estimate=cost(2**15, 2**19),
        name="spread",
    )(recv)


def inverse_factors(gram):
    row = lax.broadcasted_iota(jnp.int32, (32, 64), 0)
    lane = lax.broadcasted_iota(jnp.int32, (32, 64), 1)
    left = lane < 32
    unit = jnp.where((lane == row) | (lane == row + 32), 1.0, 0.0).astype(F32)
    scale = jnp.zeros((32, 64), F32)
    for j in range(32):
        column = jnp.where(left, gram[:, j : j + 1], gram[:, 32 + j : 33 + j])
        pivot = column[j : j + 1]
        scale = jnp.where(row == j, pivot, scale)
        share = jnp.where(row > j, column / pivot, 0.0)
        gram = gram - share * gram[j : j + 1]
        unit = unit - share * unit[j : j + 1]
    return unit / jnp.sqrt(scale)


def solve_kernel(recv, solve_out, rows_out, left_out):
    x, z, c = lax.axis_index("x"), lax.axis_index("z"), lax.axis_index("c")
    whole = recv[:, 8:24, :].reshape(NX * NZ * 16, LANES)
    square = dot(whole, whole, ((0,), (0,)))
    grams = []
    for m in range(2):
        a, b = 64 * m, 64 * m + 32
        grams.append(square[a : a + 32, a : a + 32] + square[b : b + 32, b : b + 32])
    inverse = inverse_factors(jnp.concatenate(grams, axis=1))
    blank = jnp.zeros((32, 32), F32)
    parts = [inverse[:, :32], inverse[:, 32:]]
    solve_out[...] = jnp.concatenate(
        [jnp.concatenate([parts[0], blank], axis=1), jnp.concatenate([blank, parts[1]], axis=1)],
        axis=0,
    )
    wide = jnp.concatenate(
        [
            jnp.concatenate([parts[i // 2] if i == j else blank for j in range(4)], axis=1)
            for i in range(4)
        ],
        axis=0,
    )
    mine = jnp.concatenate([recv[part * NZ + z, 8:24, :] for part in range(NX)], axis=0)
    rows = dot(mine, wide, ((1,), (1,)))
    rows_out[...] = rows
    own = rows[0:16]
    for part in range(1, NX):
        own = jnp.where(x == part, rows[16 * part : 16 * part + 16], own)
    for m in range(2):
        left_out[m] = jnp.where(c == 0, own[:, 64 * m : 64 * m + 32], own[:, 64 * m + 32 : 64 * m + 64])


def solve(recv):
    return pl.pallas_call(
        solve_kernel,
        in_specs=[VMEM],
        out_specs=[VMEM] * 3,
        out_shape=[
            jax.ShapeDtypeStruct((64, 64), F32),
            jax.ShapeDtypeStruct((64, LANES), F32),
            jax.ShapeDtypeStruct((2, 16, 32), F32),
        ],
        compiler_params=PARAMS,
        cost_estimate=cost(2**24, 2**19),
        name="solve",
    )(recv)


def approx_kernel(recv, solver, rows, send, basis_out):
    z = lax.axis_index("z")
    term = jnp.concatenate(
        [recv[a * NZ : (a + 1) * NZ].reshape(64, LANES) for a in range(8)], axis=1
    )
    turned = dot(solver[...], term, ((1,), (0,)))
    own = turned[:, :LANES]
    for a in range(1, 8):
        own = jnp.where(z == a, turned[:, a * LANES : (a + 1) * LANES], own)
    basis_out[...] = own
    for m in range(2):
        blocks = []
        for part in range(NX):
            for c in range(NC):
                at = 32 * (2 * m + c)
                blocks.append(rows[16 * part : 16 * part + 16, at : at + 32])
        result = dot(jnp.concatenate(blocks, axis=0), turned[32 * m : 32 * (m + 1)], ((1,), (0,)))
        for i in range(NX * NC):
            send[i, m] = result[16 * i : 16 * i + 16]


def approx_part(recv, solver, rows):
    return pl.pallas_call(
        approx_kernel,
        in_specs=[VMEM] * 3,
        out_specs=[VMEM] * 2,
        out_shape=[
            jax.ShapeDtypeStruct((NX * NC, 2, 16, 1024), F32),
            jax.ShapeDtypeStruct((64, LANES), F32),
        ],
        compiler_params=PARAMS,
        cost_estimate=cost(2**26, 2**20),
        name="approx_part",
    )(recv, solver, rows)


def subtract_kernel(merged, recv, out, result, sems):
    copies = []
    for x in range(NX):
        for m in range(2):
            for a in range(8):
                for c in range(NC):
                    at = pl.ds((x * 16 + 2 * a + c) * LANES, LANES)
                    approx = recv[NC * x + c, m, :, a * LANES : (a + 1) * LANES]
                    result[m, :, at] = merged[2 * a + c, x, m] - approx
        copy = pltpu.make_async_copy(
            result.at[:, :, chunk(x)], out.at[0, :, :, chunk(x)], sems.at[x]
        )
        copy.start()
        copies.append(copy)
    for copy in copies:
        copy.wait()


def subtract(merged, recv):
    _, _, mats, rows, _ = merged.shape
    width = NX * 16 * LANES
    return pl.pallas_call(
        subtract_kernel,
        in_specs=[VMEM] * 2,
        out_specs=HBM,
        out_shape=jax.ShapeDtypeStruct((1, mats, rows, width), F32),
        scratch_shapes=[pltpu.VMEM((mats, rows, width), F32), pltpu.SemaphoreType.DMA((NX,))],
        compiler_params=PARAMS,
        cost_estimate=cost(2**19, 7 * 2**19),
        name="subtract",
    )(merged, recv)


def transposition():
    far = {0: 4, 1: 3, 2: 2, 3: 1, 4: 0, 5: 7, 6: 6, 7: 5}
    pairs = []
    for a in range(8):
        for d in range(NZ):
            pairs.append((((a + far[d]) % 8) * NZ + a, a * NZ + (a + d) % NZ))
    return pairs


def shards(grads, errors, basis):
    held = basis.transpose(1, 2, 0).reshape(64, LANES)
    held = lax.ppermute(held, ("y", "z"), transposition())
    held = relay(held)
    merged = merge(grads, errors)
    recv = lax.all_to_all(merged, ("y", "c"), 0, 0)
    parts = [held] + [
        lax.ppermute(held, "x", [(i, (i + k) % NX) for i in range(NX)]) for k in range(1, NX)
    ]
    mean, send = factor_part(recv, arrange(parts))
    recv = lax.all_to_all(send, ("y", "c"), 0, 0)
    send = term_part(recv, mean)
    recv = lax.all_to_all(send, ("x", "z"), 0, 0)
    gathered = lax.all_to_all(spread(recv), ("y", "z"), 0, 0)
    solver, rows, left_factor = solve(recv)
    send, new_basis = approx_part(gathered, solver, rows)
    recv = lax.all_to_all(send, ("x", "c"), 0, 0)
    new_basis = new_basis.reshape(2, 32, LANES).transpose(2, 0, 1)
    return (subtract(merged, recv), left_factor, new_basis)


def solution(mesh):
    fine = Mesh(mesh.devices.reshape(8, NX, NZ, NC), ("y", "x", "z", "c"))
    fsdp = ("x", "z", "c")
    in_specs = (P("y", None, fsdp, None), P("y", None, fsdp, None), P(fsdp, None, None))
    out_specs = (P("y", None, fsdp, None), P(None, fsdp, None), P(fsdp, None, None))
    return jax.shard_map(shards, mesh=fine, in_specs=in_specs, out_specs=out_specs, check_vma=False)
```

```python
import jax
import jax.numpy as jnp
from jax import lax
from jax.experimental import pallas as pl
from jax.experimental.pallas import tpu as pltpu
from jax.sharding import Mesh, PartitionSpec as P

NX, NZ, NC = 4, 8, 2
LOOP = [(x, 0) for x in range(NX)] + [(x, 1) for x in reversed(range(NX))]
LANES = 128
HIGHEST = lax.Precision.HIGHEST
F32 = jnp.float32
VMEM = pl.BlockSpec(memory_space=pltpu.VMEM)
HBM = pl.BlockSpec(memory_space=pltpu.HBM)
PARAMS = pltpu.CompilerParams(vmem_limit_bytes=16 * 2**20)


def cost(flops, moved):
    return pl.CostEstimate(flops=flops, bytes_accessed=moved, transcendentals=0)


def dot(a, b, dims):
    return lax.dot_general(a, b, (dims, ((), ())), precision=HIGHEST, preferred_element_type=F32)


def chunk(x):
    return pl.ds(x * 16 * LANES, 16 * LANES)


def merge_kernel(grads, errors, out, grads_in, errors_in, blocks, sems):
    copies, results = [], []
    for x in range(NX):
        for k, (source, target) in enumerate(((grads, grads_in), (errors, errors_in))):
            copy = pltpu.make_async_copy(
                source.at[0, :, :, chunk(x)], target.at[:, :, chunk(x)], sems.at[k, x]
            )
            copy.start()
            copies.append(copy)
    for x in range(NX):
        copies[2 * x].wait()
        copies[2 * x + 1].wait()
        for m in range(2):
            for block in range(16):
                at = pl.ds((x * 16 + block) * LANES, LANES)
                blocks[block, x, m] = grads_in[m, :, at].astype(F32) + errors_in[m, :, at]
        copy = pltpu.make_async_copy(blocks.at[:, x], out.at[:, x], sems.at[2, x])
        copy.start()
        results.append(copy)
    for copy in results:
        copy.wait()


def merge(grads, errors):
    _, mats, rows, width = grads.shape
    return pl.pallas_call(
        merge_kernel,
        in_specs=[HBM] * 2,
        out_specs=HBM,
        out_shape=jax.ShapeDtypeStruct((16, NX, mats, rows, LANES), F32),
        scratch_shapes=[
            pltpu.VMEM((mats, rows, width), grads.dtype),
            pltpu.VMEM((mats, rows, width), errors.dtype),
            pltpu.VMEM((16, NX, mats, rows, LANES), F32),
            pltpu.SemaphoreType.DMA((3, NX)),
        ],
        cost_estimate=cost(2**19, 5 * 2**19),
        name="merge",
    )(grads, errors)


def relay_kernel(block, out):
    out[...] = block[...]


def relay(block):
    return pl.pallas_call(
        relay_kernel,
        in_specs=[VMEM],
        out_specs=VMEM,
        out_shape=jax.ShapeDtypeStruct(block.shape, F32),
        compiler_params=PARAMS,
        cost_estimate=cost(2**35, 2**16),
        name="relay",
    )(block)


def arrange_kernel(b0, b1, b2, b3, out):
    x = lax.axis_index("x")
    for part in range(NX):
        back = lax.rem(x - part + NX, NX)
        chosen = b0[...]
        for k, block in ((1, b1), (2, b2), (3, b3)):
            chosen = jnp.where(back == k, block[...], chosen)
        out[:, part * LANES : (part + 1) * LANES] = chosen


def arrange(shards):
    return pl.pallas_call(
        arrange_kernel,
        in_specs=[VMEM] * 4,
        out_specs=VMEM,
        out_shape=jax.ShapeDtypeStruct((64, NX * LANES), F32),
        compiler_params=PARAMS,
        cost_estimate=cost(2**20, 2**18),
        name="arrange",
    )(*shards)


def factor_kernel(recv, weights, mean_out, send):
    columns = []
    for part in range(NX):
        blocks = []
        for m in range(2):
            for c in range(NC):
                total = recv[c, part, m]
                for a in range(1, 8):
                    total = total + recv[2 * a + c, part, m]
                blocks.append(total)
        columns.append(jnp.concatenate(blocks, axis=0) * 0.125)
    mean = jnp.concatenate(columns, axis=1)
    mean_out[...] = mean
    partial = dot(mean, weights[...], ((1,), (1,)))
    piece = jnp.concatenate(
        [
            partial[16 * (2 * m + c) : 16 * (2 * m + c + 1), 32 * m : 32 * (m + 1)]
            for m in range(2)
            for c in range(NC)
        ],
        axis=1,
    )
    for i in range(16):
        send[i] = piece


def factor_part(recv, weights):
    return pl.pallas_call(
        factor_kernel,
        in_specs=[VMEM] * 2,
        out_specs=[VMEM] * 2,
        out_shape=[
            jax.ShapeDtypeStruct((64, 512), F32),
            jax.ShapeDtypeStruct((16, 16, LANES), F32),
        ],
        compiler_params=PARAMS,
        cost_estimate=cost(2**22, 2**20 + 2**19),
        name="factor_part",
    )(recv, weights)


def term_kernel(recv, mean, send):
    factor = recv[0]
    for i in range(1, 16):
        factor = factor + recv[i]
    blank = jnp.zeros((16, 32), F32)
    rows = []
    for m in range(2):
        for c in range(NC):
            piece = factor[:, 32 * (2 * m + c) : 32 * (2 * m + c + 1)]
            rows.append(jnp.concatenate([piece, blank] if m == 0 else [blank, piece], axis=1))
    blocked = jnp.concatenate(rows, axis=0)
    half = jnp.where(lax.axis_index("c") == 0, factor[:, :64], factor[:, 64:])
    half = jnp.concatenate([half[:8], half[8:]], axis=1)
    term = dot(blocked, mean[...], ((0,), (0,)))
    for x in range(NX):
        for z in range(NZ):
            send[x * NZ + z, 0:8] = term[8 * z : 8 * z + 8, x * LANES : (x + 1) * LANES]
            send[x * NZ + z, 8:16] = half


def term_part(recv, mean):
    return pl.pallas_call(
        term_kernel,
        in_specs=[VMEM] * 2,
        out_specs=VMEM,
        out_shape=jax.ShapeDtypeStruct((NX * NZ, 16, LANES), F32),
        compiler_params=PARAMS,
        cost_estimate=cost(2**23, 2**20),
        name="term_part",
    )(recv, mean)


def spread_kernel(recv, send):
    total = recv[0, 0:8]
    for g in range(1, NX * NZ):
        total = total + recv[g, 0:8]
    for i in range(8 * NZ):
        send[i] = total


def spread(recv):
    return pl.pallas_call(
        spread_kernel,
        in_specs=[VMEM],
        out_specs=VMEM,
        out_shape=jax.ShapeDtypeStruct((8 * NZ, 8, LANES), F32),
        compiler_params=PARAMS,
        cost_estimate=cost(2**15, 2**19),
        name="spread",
    )(recv)


def inverse_factor(gram):
    row = lax.broadcasted_iota(jnp.int32, (32, 32), 0)
    lane = lax.broadcasted_iota(jnp.int32, (32, 32), 1)
    unit = jnp.where(lane == row, 1.0, 0.0).astype(F32)
    scale = jnp.zeros((32, 32), F32)
    for j in range(32):
        column = gram[:, j : j + 1]
        pivot = column[j : j + 1]
        scale = jnp.where(row == j, pivot, scale)
        share = jnp.where(row > j, column / pivot, 0.0)
        gram = gram - share * gram[j : j + 1]
        unit = unit - share * unit[j : j + 1]
    return unit / jnp.sqrt(scale)


def solve_kernel(recv, out):
    z = lax.axis_index("z")
    packed = recv[:, 8:16, :].reshape(NX * NZ * 8, LANES)
    low, high = packed[:, :64], packed[:, 64:]
    square = dot(low, low, ((0,), (0,))) + dot(high, high, ((0,), (0,)))
    inverse = inverse_factor(square[:32, :32] + square[32:, 32:])
    blank = jnp.zeros((32, 32), F32)
    wide = jnp.concatenate(
        [jnp.concatenate([inverse, blank], axis=1), jnp.concatenate([blank, inverse], axis=1)],
        axis=0,
    )
    mine = []
    for part in range(NX):
        block = recv[part * NZ + z, 8:16]
        mine += [block[:, :64], block[:, 64:]]
    out[:, :64] = dot(jnp.concatenate(mine, axis=0), wide, ((1,), (1,)))
    out[:, 64:] = wide


def solve(recv):
    return pl.pallas_call(
        solve_kernel,
        in_specs=[VMEM],
        out_specs=VMEM,
        out_shape=jax.ShapeDtypeStruct((64, LANES), F32),
        compiler_params=PARAMS,
        cost_estimate=cost(2**24, 2**19),
        name="solve",
    )(recv)


def approx_kernel(recv, mine, other, send, basis_out, left_out):
    x, z, c = lax.axis_index("x"), lax.axis_index("z"), lax.axis_index("c")
    for m in range(2):
        solved = jnp.where(c == m, mine[...], other[...])
        term = jnp.concatenate(
            [recv[a * NZ + 4 * m : a * NZ + 4 * m + 4].reshape(32, LANES) for a in range(8)], axis=1
        )
        turned = dot(solved[:32, 64:96], term, ((1,), (0,)))
        own = turned[:, :LANES]
        for a in range(1, 8):
            own = jnp.where(z == a, turned[:, a * LANES : (a + 1) * LANES], own)
        basis_out[32 * m : 32 * (m + 1)] = own
        rows = [solved[16 * at : 16 * at + 16, 32 * core : 32 * core + 32] for at, core in LOOP]
        left = rows[0]
        for i, (at, core) in enumerate(LOOP):
            left = jnp.where((x == at) & (c == core), rows[i], left)
        left_out[m] = left
        result = dot(jnp.concatenate(rows, axis=0), turned, ((1,), (0,)))
        for i in range(NX * NC):
            send[i, m] = result[16 * i : 16 * i + 16]


def approx_part(recv, mine, other):
    return pl.pallas_call(
        approx_kernel,
        in_specs=[VMEM] * 3,
        out_specs=[VMEM] * 3,
        out_shape=[
            jax.ShapeDtypeStruct((NX * NC, 2, 16, 1024), F32),
            jax.ShapeDtypeStruct((64, LANES), F32),
            jax.ShapeDtypeStruct((2, 16, 32), F32),
        ],
        compiler_params=PARAMS,
        cost_estimate=cost(2**26, 2**20),
        name="approx_part",
    )(recv, mine, other)


def subtract_kernel(merged, recv, out, result, sems):
    copies = []
    for x in range(NX):
        for m in range(2):
            for a in range(8):
                for c in range(NC):
                    at = pl.ds((x * 16 + 2 * a + c) * LANES, LANES)
                    approx = recv[LOOP.index((x, c)), m, :, a * LANES : (a + 1) * LANES]
                    result[m, :, at] = merged[2 * a + c, x, m] - approx
        copy = pltpu.make_async_copy(
            result.at[:, :, chunk(x)], out.at[0, :, :, chunk(x)], sems.at[x]
        )
        copy.start()
        copies.append(copy)
    for copy in copies:
        copy.wait()


def subtract(merged, recv):
    _, _, mats, rows, _ = merged.shape
    width = NX * 16 * LANES
    return pl.pallas_call(
        subtract_kernel,
        in_specs=[VMEM] * 2,
        out_specs=HBM,
        out_shape=jax.ShapeDtypeStruct((1, mats, rows, width), F32),
        scratch_shapes=[pltpu.VMEM((mats, rows, width), F32), pltpu.SemaphoreType.DMA((NX,))],
        compiler_params=PARAMS,
        cost_estimate=cost(2**19, 7 * 2**19),
        name="subtract",
    )(merged, recv)


def transposition():
    far = {0: 4, 1: 3, 2: 2, 3: 1, 4: 0, 5: 7, 6: 6, 7: 5}
    pairs = []
    for a in range(8):
        for d in range(NZ):
            pairs.append((((a + far[d]) % 8) * NZ + a, a * NZ + (a + d) % NZ))
    return pairs


def shards(grads, errors, basis):
    held = basis.transpose(1, 2, 0).reshape(64, LANES)
    held = lax.ppermute(held, ("y", "z"), transposition())
    held = relay(held)
    merged = merge(grads, errors)
    recv = lax.all_to_all(merged, ("y", "c"), 0, 0)
    parts = [held] + [
        lax.ppermute(held, "x", [(i, (i + k) % NX) for i in range(NX)]) for k in range(1, NX)
    ]
    mean, send = factor_part(recv, arrange(parts))
    recv = lax.all_to_all(send, ("y", "c"), 0, 0)
    send = term_part(recv, mean)
    recv = lax.all_to_all(send, ("x", "z"), 0, 0)
    gathered = lax.all_to_all(spread(recv), ("y", "z"), 0, 0)
    mine = solve(recv)
    other = lax.ppermute(mine, "c", [(0, 1), (1, 0)])
    send, new_basis, left_factor = approx_part(gathered, mine, other)
    groups = [[x * NC + c for x, c in LOOP]]
    recv = lax.all_to_all(send, ("x", "c"), 0, 0, axis_index_groups=groups)
    new_basis = new_basis.reshape(2, 32, LANES).transpose(2, 0, 1)
    return (subtract(merged, recv), left_factor, new_basis)


def solution(mesh):
    fine = Mesh(mesh.devices.reshape(8, NX, NZ, NC), ("y", "x", "z", "c"))
    fsdp = ("x", "z", "c")
    in_specs = (P("y", None, fsdp, None), P("y", None, fsdp, None), P(fsdp, None, None))
    out_specs = (P("y", None, fsdp, None), P(None, fsdp, None), P(fsdp, None, None))
    return jax.shard_map(shards, mesh=fine, in_specs=in_specs, out_specs=out_specs, check_vma=False)
```

```python
import jax
import jax.numpy as jnp
from jax import lax
from jax.experimental import pallas as pl
from jax.experimental.pallas import tpu as pltpu
from jax.sharding import Mesh, PartitionSpec as P

NX, NZ, NC = 4, 8, 2
LOOP = [(x, 0) for x in range(NX)] + [(x, 1) for x in reversed(range(NX))]
LANES = 128
HIGHEST = lax.Precision.HIGHEST
F32 = jnp.float32
VMEM = pl.BlockSpec(memory_space=pltpu.VMEM)
HBM = pl.BlockSpec(memory_space=pltpu.HBM)
PARAMS = pltpu.CompilerParams(vmem_limit_bytes=16 * 2**20)


def cost(flops, moved):
    return pl.CostEstimate(flops=flops, bytes_accessed=moved, transcendentals=0)


def dot(a, b, dims):
    return lax.dot_general(a, b, (dims, ((), ())), precision=HIGHEST, preferred_element_type=F32)


def chunk(x):
    return pl.ds(x * 16 * LANES, 16 * LANES)


def merge_kernel(grads, errors, out, grads_in, errors_in, blocks, sems):
    copies, results = [], []
    for x in range(NX):
        for k, (source, target) in enumerate(((grads, grads_in), (errors, errors_in))):
            copy = pltpu.make_async_copy(
                source.at[0, :, :, chunk(x)], target.at[:, :, chunk(x)], sems.at[k, x]
            )
            copy.start()
            copies.append(copy)
    for x in range(NX):
        copies[2 * x].wait()
        copies[2 * x + 1].wait()
        for m in range(2):
            for block in range(16):
                at = pl.ds((x * 16 + block) * LANES, LANES)
                blocks[block, x, m] = grads_in[m, :, at].astype(F32) + errors_in[m, :, at]
        copy = pltpu.make_async_copy(blocks.at[:, x], out.at[:, x], sems.at[2, x])
        copy.start()
        results.append(copy)
    for copy in results:
        copy.wait()


def merge(grads, errors):
    _, mats, rows, width = grads.shape
    return pl.pallas_call(
        merge_kernel,
        in_specs=[HBM] * 2,
        out_specs=HBM,
        out_shape=jax.ShapeDtypeStruct((16, NX, mats, rows, LANES), F32),
        scratch_shapes=[
            pltpu.VMEM((mats, rows, width), grads.dtype),
            pltpu.VMEM((mats, rows, width), errors.dtype),
            pltpu.VMEM((16, NX, mats, rows, LANES), F32),
            pltpu.SemaphoreType.DMA((3, NX)),
        ],
        cost_estimate=cost(2**19, 5 * 2**19),
        name="merge",
    )(grads, errors)


def relay_kernel(block, out):
    out[...] = block[...]


def relay(block):
    return pl.pallas_call(
        relay_kernel,
        in_specs=[VMEM],
        out_specs=VMEM,
        out_shape=jax.ShapeDtypeStruct(block.shape, F32),
        compiler_params=PARAMS,
        cost_estimate=cost(2**35, 2**16),
        name="relay",
    )(block)


def arrange_kernel(b0, b1, b2, b3, out):
    x = lax.axis_index("x")
    for part in range(NX):
        back = lax.rem(x - part + NX, NX)
        chosen = b0[...]
        for k, block in ((1, b1), (2, b2), (3, b3)):
            chosen = jnp.where(back == k, block[...], chosen)
        out[:, part * LANES : (part + 1) * LANES] = chosen


def arrange(shards):
    return pl.pallas_call(
        arrange_kernel,
        in_specs=[VMEM] * 4,
        out_specs=VMEM,
        out_shape=jax.ShapeDtypeStruct((64, NX * LANES), F32),
        compiler_params=PARAMS,
        cost_estimate=cost(2**20, 2**18),
        name="arrange",
    )(*shards)


def factor_kernel(recv, weights, mean_out, send):
    columns = []
    for part in range(NX):
        blocks = []
        for m in range(2):
            for c in range(NC):
                total = recv[c, part, m]
                for a in range(1, 8):
                    total = total + recv[2 * a + c, part, m]
                blocks.append(total)
        columns.append(jnp.concatenate(blocks, axis=0) * 0.125)
    mean = jnp.concatenate(columns, axis=1)
    mean_out[...] = mean
    partial = dot(mean, weights[...], ((1,), (1,)))
    piece = jnp.concatenate(
        [
            partial[16 * (2 * m + c) : 16 * (2 * m + c + 1), 32 * m : 32 * (m + 1)]
            for m in range(2)
            for c in range(NC)
        ],
        axis=1,
    )
    for i in range(16):
        send[i] = piece


def factor_part(recv, weights):
    return pl.pallas_call(
        factor_kernel,
        in_specs=[VMEM] * 2,
        out_specs=[VMEM] * 2,
        out_shape=[
            jax.ShapeDtypeStruct((64, 512), F32),
            jax.ShapeDtypeStruct((16, 16, LANES), F32),
        ],
        compiler_params=PARAMS,
        cost_estimate=cost(2**22, 2**20 + 2**19),
        name="factor_part",
    )(recv, weights)


def term_kernel(recv, mean, send):
    factor = recv[0]
    for i in range(1, 16):
        factor = factor + recv[i]
    blank = jnp.zeros((16, 32), F32)
    rows = []
    for m in range(2):
        for c in range(NC):
            piece = factor[:, 32 * (2 * m + c) : 32 * (2 * m + c + 1)]
            rows.append(jnp.concatenate([piece, blank] if m == 0 else [blank, piece], axis=1))
    blocked = jnp.concatenate(rows, axis=0)
    half = jnp.where(lax.axis_index("c") == 0, factor[:, :64], factor[:, 64:])
    half = jnp.concatenate([half[:8], half[8:]], axis=1)
    term = dot(blocked, mean[...], ((0,), (0,)))
    for x in range(NX):
        for z in range(NZ):
            send[x * NZ + z, 0:8] = term[8 * z : 8 * z + 8, x * LANES : (x + 1) * LANES]
            send[x * NZ + z, 8:16] = half


def term_part(recv, mean):
    return pl.pallas_call(
        term_kernel,
        in_specs=[VMEM] * 2,
        out_specs=VMEM,
        out_shape=jax.ShapeDtypeStruct((NX * NZ, 16, LANES), F32),
        compiler_params=PARAMS,
        cost_estimate=cost(2**23, 2**20),
        name="term_part",
    )(recv, mean)


def spread_kernel(recv, send):
    total = recv[0, 0:8]
    for g in range(1, NX * NZ):
        total = total + recv[g, 0:8]
    for i in range(8 * NZ):
        send[i] = total


def spread(recv):
    return pl.pallas_call(
        spread_kernel,
        in_specs=[VMEM],
        out_specs=VMEM,
        out_shape=jax.ShapeDtypeStruct((8 * NZ, 8, LANES), F32),
        compiler_params=PARAMS,
        cost_estimate=cost(2**15, 2**19),
        name="spread",
    )(recv)


def inverse_factor(gram):
    row = lax.broadcasted_iota(jnp.int32, (32, 32), 0)
    lane = lax.broadcasted_iota(jnp.int32, (32, 32), 1)
    unit = jnp.where(lane == row, 1.0, 0.0).astype(F32)
    scale = jnp.zeros((32, 32), F32)
    for j in range(32):
        column = gram[:, j : j + 1]
        pivot = column[j : j + 1]
        scale = jnp.where(row == j, pivot, scale)
        share = jnp.where(row > j, column / pivot, 0.0)
        gram = gram - share * gram[j : j + 1]
        unit = unit - share * unit[j : j + 1]
    return unit / jnp.sqrt(scale)


def solve_kernel(recv, out):
    z = lax.axis_index("z")
    packed = recv[:, 8:16, :].reshape(NX * NZ * 8, LANES)
    low, high = packed[:, :64], packed[:, 64:]
    square = dot(low, low, ((0,), (0,))) + dot(high, high, ((0,), (0,)))
    inverse = inverse_factor(square[:32, :32] + square[32:, 32:])
    blank = jnp.zeros((32, 32), F32)
    wide = jnp.concatenate(
        [jnp.concatenate([inverse, blank], axis=1), jnp.concatenate([blank, inverse], axis=1)],
        axis=0,
    )
    mine = []
    for part in range(NX):
        block = recv[part * NZ + z, 8:16]
        mine += [block[:, :64], block[:, 64:]]
    out[:, :64] = dot(jnp.concatenate(mine, axis=0), wide, ((1,), (1,)))
    out[:, 64:] = wide


def solve(recv):
    return pl.pallas_call(
        solve_kernel,
        in_specs=[VMEM],
        out_specs=VMEM,
        out_shape=jax.ShapeDtypeStruct((64, LANES), F32),
        compiler_params=PARAMS,
        cost_estimate=cost(2**24, 2**19),
        name="solve",
    )(recv)


def solutions(mine, other):
    c = lax.axis_index("c")
    solved = [jnp.where(c == m, mine[...], other[...]) for m in range(2)]
    blank = jnp.zeros((32, 32), F32)
    inverse = jnp.concatenate(
        [
            jnp.concatenate([solved[0][:32, 64:96], blank], axis=1),
            jnp.concatenate([blank, solved[1][:32, 64:96]], axis=1),
        ],
        axis=0,
    )
    rows = [
        [solved[m][16 * x : 16 * x + 16, 32 * c : 32 * c + 32] for x, c in LOOP] for m in range(2)
    ]
    return inverse, rows


def approx_kernel(recv, mine, other, send):
    inverse, rows = solutions(mine, other)
    term = jnp.concatenate(
        [recv[a * NZ : (a + 1) * NZ].reshape(64, LANES) for a in range(8)], axis=1
    )
    turned = dot(inverse, term, ((1,), (0,)))
    for m in range(2):
        result = dot(jnp.concatenate(rows[m], axis=0), turned[32 * m : 32 * (m + 1)], ((1,), (0,)))
        for i in range(NX * NC):
            send[i, m] = result[16 * i : 16 * i + 16]


def approx_part(recv, mine, other):
    return pl.pallas_call(
        approx_kernel,
        in_specs=[VMEM] * 3,
        out_specs=VMEM,
        out_shape=jax.ShapeDtypeStruct((NX * NC, 2, 16, 1024), F32),
        compiler_params=PARAMS,
        cost_estimate=cost(2**26, 2**20),
        name="approx_part",
    )(recv, mine, other)


def outputs_kernel(recv, mine, other, basis_out, left_out):
    x, z, c = lax.axis_index("x"), lax.axis_index("z"), lax.axis_index("c")
    inverse, rows = solutions(mine, other)
    own = recv[pl.ds(z * NZ, NZ)].reshape(64, LANES)
    basis_out[...] = dot(inverse, own, ((1,), (0,)))
    for m in range(2):
        left = rows[m][0]
        for i, (at, core) in enumerate(LOOP):
            left = jnp.where((x == at) & (c == core), rows[m][i], left)
        left_out[m] = left


def outputs(recv, mine, other):
    return pl.pallas_call(
        outputs_kernel,
        in_specs=[VMEM] * 3,
        out_specs=[VMEM] * 2,
        out_shape=[
            jax.ShapeDtypeStruct((64, LANES), F32),
            jax.ShapeDtypeStruct((2, 16, 32), F32),
        ],
        compiler_params=PARAMS,
        cost_estimate=cost(2**24, 2**19),
        name="outputs",
    )(recv, mine, other)


def subtract_kernel(merged, recv, out, result, sems):
    copies = []
    for x in range(NX):
        for m in range(2):
            for a in range(8):
                for c in range(NC):
                    at = pl.ds((x * 16 + 2 * a + c) * LANES, LANES)
                    approx = recv[LOOP.index((x, c)), m, :, a * LANES : (a + 1) * LANES]
                    result[m, :, at] = merged[2 * a + c, x, m] - approx
        copy = pltpu.make_async_copy(
            result.at[:, :, chunk(x)], out.at[0, :, :, chunk(x)], sems.at[x]
        )
        copy.start()
        copies.append(copy)
    for copy in copies:
        copy.wait()


def subtract(merged, recv):
    _, _, mats, rows, _ = merged.shape
    width = NX * 16 * LANES
    return pl.pallas_call(
        subtract_kernel,
        in_specs=[VMEM] * 2,
        out_specs=HBM,
        out_shape=jax.ShapeDtypeStruct((1, mats, rows, width), F32),
        scratch_shapes=[pltpu.VMEM((mats, rows, width), F32), pltpu.SemaphoreType.DMA((NX,))],
        compiler_params=PARAMS,
        cost_estimate=cost(2**19, 7 * 2**19),
        name="subtract",
    )(merged, recv)


def transposition():
    far = {0: 4, 1: 3, 2: 2, 3: 1, 4: 0, 5: 7, 6: 6, 7: 5}
    pairs = []
    for a in range(8):
        for d in range(NZ):
            pairs.append((((a + far[d]) % 8) * NZ + a, a * NZ + (a + d) % NZ))
    return pairs


def shards(grads, errors, basis):
    held = basis.transpose(1, 2, 0).reshape(64, LANES)
    held = lax.ppermute(held, ("y", "z"), transposition())
    held = relay(held)
    merged = merge(grads, errors)
    recv = lax.all_to_all(merged, ("y", "c"), 0, 0)
    parts = [held] + [
        lax.ppermute(held, "x", [(i, (i + k) % NX) for i in range(NX)]) for k in range(1, NX)
    ]
    mean, send = factor_part(recv, arrange(parts))
    recv = lax.all_to_all(send, ("y", "c"), 0, 0)
    send = term_part(recv, mean)
    recv = lax.all_to_all(send, ("x", "z"), 0, 0)
    gathered = lax.all_to_all(spread(recv), ("y", "z"), 0, 0)
    mine = solve(recv)
    other = lax.ppermute(mine, "c", [(0, 1), (1, 0)])
    send = approx_part(gathered, mine, other)
    new_basis, left_factor = outputs(gathered, mine, other)
    groups = [[x * NC + c for x, c in LOOP]]
    recv = lax.all_to_all(send, ("x", "c"), 0, 0, axis_index_groups=groups)
    new_basis = new_basis.reshape(2, 32, LANES).transpose(2, 0, 1)
    return (subtract(merged, recv), left_factor, new_basis)


def solution(mesh):
    fine = Mesh(mesh.devices.reshape(8, NX, NZ, NC), ("y", "x", "z", "c"))
    fsdp = ("x", "z", "c")
    in_specs = (P("y", None, fsdp, None), P("y", None, fsdp, None), P(fsdp, None, None))
    out_specs = (P("y", None, fsdp, None), P(None, fsdp, None), P(fsdp, None, None))
    return jax.shard_map(shards, mesh=fine, in_specs=in_specs, out_specs=out_specs, check_vma=False)
```

```python
import jax
import jax.numpy as jnp
from jax import lax
from jax.experimental import pallas as pl
from jax.experimental.pallas import tpu as pltpu
from jax.sharding import Mesh, PartitionSpec as P

NX, NZ, NC = 4, 8, 2
LOOP = [(x, 0) for x in range(NX)] + [(x, 1) for x in reversed(range(NX))]
LANES = 128
HIGHEST = lax.Precision.HIGHEST
F32 = jnp.float32
VMEM = pl.BlockSpec(memory_space=pltpu.VMEM)
HBM = pl.BlockSpec(memory_space=pltpu.HBM)
PARAMS = pltpu.CompilerParams(vmem_limit_bytes=16 * 2**20)


def cost(flops, moved):
    return pl.CostEstimate(flops=flops, bytes_accessed=moved, transcendentals=0)


def dot(a, b, dims):
    return lax.dot_general(a, b, (dims, ((), ())), precision=HIGHEST, preferred_element_type=F32)


def chunk(x):
    return pl.ds(x * 16 * LANES, 16 * LANES)


def merge_kernel(grads, errors, out, grads_in, errors_in, blocks, sems):
    copies, results = [], []
    for x in range(NX):
        for k, (source, target) in enumerate(((grads, grads_in), (errors, errors_in))):
            copy = pltpu.make_async_copy(
                source.at[0, :, :, chunk(x)], target.at[:, :, chunk(x)], sems.at[k, x]
            )
            copy.start()
            copies.append(copy)
    for x in range(NX):
        copies[2 * x].wait()
        copies[2 * x + 1].wait()
        for m in range(2):
            for block in range(16):
                at = pl.ds((x * 16 + block) * LANES, LANES)
                blocks[block, x, m] = grads_in[m, :, at].astype(F32) + errors_in[m, :, at]
        copy = pltpu.make_async_copy(blocks.at[:, x], out.at[:, x], sems.at[2, x])
        copy.start()
        results.append(copy)
    for copy in results:
        copy.wait()


def merge(grads, errors):
    _, mats, rows, width = grads.shape
    return pl.pallas_call(
        merge_kernel,
        in_specs=[HBM] * 2,
        out_specs=HBM,
        out_shape=jax.ShapeDtypeStruct((16, NX, mats, rows, LANES), F32),
        scratch_shapes=[
            pltpu.VMEM((mats, rows, width), grads.dtype),
            pltpu.VMEM((mats, rows, width), errors.dtype),
            pltpu.VMEM((16, NX, mats, rows, LANES), F32),
            pltpu.SemaphoreType.DMA((3, NX)),
        ],
        cost_estimate=cost(2**19, 5 * 2**19),
        name="merge",
    )(grads, errors)


def relay_kernel(block, out):
    out[...] = block[...]


def relay(block):
    return pl.pallas_call(
        relay_kernel,
        in_specs=[VMEM],
        out_specs=VMEM,
        out_shape=jax.ShapeDtypeStruct(block.shape, F32),
        compiler_params=PARAMS,
        cost_estimate=cost(2**35, 2**16),
        name="relay",
    )(block)


def arrange_kernel(b0, b1, b2, b3, out):
    x = lax.axis_index("x")
    for part in range(NX):
        back = lax.rem(x - part + NX, NX)
        chosen = b0[...]
        for k, block in ((1, b1), (2, b2), (3, b3)):
            chosen = jnp.where(back == k, block[...], chosen)
        out[:, part * LANES : (part + 1) * LANES] = chosen


def arrange(shards):
    return pl.pallas_call(
        arrange_kernel,
        in_specs=[VMEM] * 4,
        out_specs=VMEM,
        out_shape=jax.ShapeDtypeStruct((64, NX * LANES), F32),
        compiler_params=PARAMS,
        cost_estimate=cost(2**20, 2**18),
        name="arrange",
    )(*shards)


def factor_kernel(recv, weights, mean_out, send):
    columns = []
    for part in range(NX):
        blocks = []
        for m in range(2):
            for c in range(NC):
                total = recv[c, part, m]
                for a in range(1, 8):
                    total = total + recv[2 * a + c, part, m]
                blocks.append(total)
        columns.append(jnp.concatenate(blocks, axis=0) * 0.125)
    mean = jnp.concatenate(columns, axis=1)
    mean_out[...] = mean
    partial = dot(mean, weights[...], ((1,), (1,)))
    piece = jnp.concatenate(
        [
            partial[16 * (2 * m + c) : 16 * (2 * m + c + 1), 32 * m : 32 * (m + 1)]
            for m in range(2)
            for c in range(NC)
        ],
        axis=1,
    )
    for i in range(16):
        send[i] = piece


def factor_part(recv, weights):
    return pl.pallas_call(
        factor_kernel,
        in_specs=[VMEM] * 2,
        out_specs=[VMEM] * 2,
        out_shape=[
            jax.ShapeDtypeStruct((64, 512), F32),
            jax.ShapeDtypeStruct((16, 16, LANES), F32),
        ],
        compiler_params=PARAMS,
        cost_estimate=cost(2**22, 2**20 + 2**19),
        name="factor_part",
    )(recv, weights)


def term_kernel(recv, mean, send):
    factor = recv[0]
    for i in range(1, 16):
        factor = factor + recv[i]
    blank = jnp.zeros((16, 32), F32)
    rows = []
    for m in range(2):
        for c in range(NC):
            piece = factor[:, 32 * (2 * m + c) : 32 * (2 * m + c + 1)]
            rows.append(jnp.concatenate([piece, blank] if m == 0 else [blank, piece], axis=1))
    blocked = jnp.concatenate(rows, axis=0)
    half = jnp.where(lax.axis_index("c") == 0, factor[:, :64], factor[:, 64:])
    half = jnp.concatenate([half[:8], half[8:]], axis=1)
    term = dot(blocked, mean[...], ((0,), (0,)))
    for x in range(NX):
        for z in range(NZ):
            send[x * NZ + z, 0:8] = term[8 * z : 8 * z + 8, x * LANES : (x + 1) * LANES]
            send[x * NZ + z, 8:16] = half


def term_part(recv, mean):
    return pl.pallas_call(
        term_kernel,
        in_specs=[VMEM] * 2,
        out_specs=VMEM,
        out_shape=jax.ShapeDtypeStruct((NX * NZ, 16, LANES), F32),
        compiler_params=PARAMS,
        cost_estimate=cost(2**23, 2**20),
        name="term_part",
    )(recv, mean)


def spread_kernel(recv, send):
    total = recv[0, 0:8]
    for g in range(1, NX * NZ):
        total = total + recv[g, 0:8]
    for i in range(8 * NZ):
        send[i] = total


def spread(recv):
    return pl.pallas_call(
        spread_kernel,
        in_specs=[VMEM],
        out_specs=VMEM,
        out_shape=jax.ShapeDtypeStruct((8 * NZ, 8, LANES), F32),
        compiler_params=PARAMS,
        cost_estimate=cost(2**15, 2**19),
        name="spread",
    )(recv)


def inverse_factor(gram):
    row = lax.broadcasted_iota(jnp.int32, (32, 32), 0)
    lane = lax.broadcasted_iota(jnp.int32, (32, 32), 1)
    unit = jnp.where(lane == row, 1.0, 0.0).astype(F32)
    scale = jnp.zeros((32, 32), F32)
    for j in range(32):
        column = gram[:, j : j + 1]
        pivot = column[j : j + 1]
        scale = jnp.where(row == j, pivot, scale)
        share = jnp.where(row > j, column / pivot, 0.0)
        gram = gram - share * gram[j : j + 1]
        unit = unit - share * unit[j : j + 1]
    return unit / jnp.sqrt(scale)


def solve_kernel(recv, out):
    z = lax.axis_index("z")
    packed = recv[:, 8:16, :].reshape(NX * NZ * 8, LANES)
    low, high = packed[:, :64], packed[:, 64:]
    square = dot(low, low, ((0,), (0,))) + dot(high, high, ((0,), (0,)))
    inverse = inverse_factor(square[:32, :32] + square[32:, 32:])
    blank = jnp.zeros((32, 32), F32)
    wide = jnp.concatenate(
        [jnp.concatenate([inverse, blank], axis=1), jnp.concatenate([blank, inverse], axis=1)],
        axis=0,
    )
    mine = []
    for part in range(NX):
        block = recv[part * NZ + z, 8:16]
        mine += [block[:, :64], block[:, 64:]]
    out[:, :64] = dot(jnp.concatenate(mine, axis=0), wide, ((1,), (1,)))
    out[:, 64:] = wide


def solve(recv):
    return pl.pallas_call(
        solve_kernel,
        in_specs=[VMEM],
        out_specs=VMEM,
        out_shape=jax.ShapeDtypeStruct((64, LANES), F32),
        compiler_params=PARAMS,
        cost_estimate=cost(2**24, 2**19),
        name="solve",
    )(recv)


def solutions(mine, other):
    c = lax.axis_index("c")
    solved = [jnp.where(c == m, mine[...], other[...]) for m in range(2)]
    blank = jnp.zeros((32, 32), F32)
    inverse = jnp.concatenate(
        [
            jnp.concatenate([solved[0][:32, 64:96], blank], axis=1),
            jnp.concatenate([blank, solved[1][:32, 64:96]], axis=1),
        ],
        axis=0,
    )
    rows = [
        [solved[m][16 * x : 16 * x + 16, 32 * c : 32 * c + 32] for x, c in LOOP] for m in range(2)
    ]
    return inverse, rows


def approx_kernel(recv, mine, other, send, basis_out):
    z = lax.axis_index("z")
    inverse, rows = solutions(mine, other)
    term = jnp.concatenate(
        [recv[a * NZ : (a + 1) * NZ].reshape(64, LANES) for a in range(8)], axis=1
    )
    turned = dot(inverse, term, ((1,), (0,)))
    own = turned[:, :LANES]
    for a in range(1, 8):
        own = jnp.where(z == a, turned[:, a * LANES : (a + 1) * LANES], own)
    basis_out[...] = own
    for m in range(2):
        result = dot(jnp.concatenate(rows[m], axis=0), turned[32 * m : 32 * (m + 1)], ((1,), (0,)))
        for i in range(NX * NC):
            send[i, m] = result[16 * i : 16 * i + 16]


def approx_part(recv, mine, other):
    return pl.pallas_call(
        approx_kernel,
        in_specs=[VMEM] * 3,
        out_specs=[VMEM] * 2,
        out_shape=[
            jax.ShapeDtypeStruct((NX * NC, 2, 16, 1024), F32),
            jax.ShapeDtypeStruct((64, LANES), F32),
        ],
        compiler_params=PARAMS,
        cost_estimate=cost(2**26, 2**20),
        name="approx_part",
    )(recv, mine, other)


def left_kernel(mine, other, out):
    x, c = lax.axis_index("x"), lax.axis_index("c")
    _, rows = solutions(mine, other)
    for m in range(2):
        left = rows[m][0]
        for i, (at, core) in enumerate(LOOP):
            left = jnp.where((x == at) & (c == core), rows[m][i], left)
        out[m] = left


def left_part(mine, other):
    return pl.pallas_call(
        left_kernel,
        in_specs=[VMEM] * 2,
        out_specs=VMEM,
        out_shape=jax.ShapeDtypeStruct((2, 16, 32), F32),
        compiler_params=PARAMS,
        cost_estimate=cost(2**22, 2**17),
        name="left_part",
    )(mine, other)


def subtract_kernel(merged, recv, out, result, sems):
    copies = []
    for x in range(NX):
        for m in range(2):
            for a in range(8):
                for c in range(NC):
                    at = pl.ds((x * 16 + 2 * a + c) * LANES, LANES)
                    approx = recv[LOOP.index((x, c)), m, :, a * LANES : (a + 1) * LANES]
                    result[m, :, at] = merged[2 * a + c, x, m] - approx
        copy = pltpu.make_async_copy(
            result.at[:, :, chunk(x)], out.at[0, :, :, chunk(x)], sems.at[x]
        )
        copy.start()
        copies.append(copy)
    for copy in copies:
        copy.wait()


def subtract(merged, recv):
    _, _, mats, rows, _ = merged.shape
    width = NX * 16 * LANES
    return pl.pallas_call(
        subtract_kernel,
        in_specs=[VMEM] * 2,
        out_specs=HBM,
        out_shape=jax.ShapeDtypeStruct((1, mats, rows, width), F32),
        scratch_shapes=[pltpu.VMEM((mats, rows, width), F32), pltpu.SemaphoreType.DMA((NX,))],
        compiler_params=PARAMS,
        cost_estimate=cost(2**19, 7 * 2**19),
        name="subtract",
    )(merged, recv)


def transposition():
    far = {0: 4, 1: 3, 2: 2, 3: 1, 4: 0, 5: 7, 6: 6, 7: 5}
    pairs = []
    for a in range(8):
        for d in range(NZ):
            pairs.append((((a + far[d]) % 8) * NZ + a, a * NZ + (a + d) % NZ))
    return pairs


def shards(grads, errors, basis):
    held = basis.transpose(1, 2, 0).reshape(64, LANES)
    held = lax.ppermute(held, ("y", "z"), transposition())
    held = relay(held)
    merged = merge(grads, errors)
    recv = lax.all_to_all(merged, ("y", "c"), 0, 0)
    parts = [held] + [
        lax.ppermute(held, "x", [(i, (i + k) % NX) for i in range(NX)]) for k in range(1, NX)
    ]
    mean, send = factor_part(recv, arrange(parts))
    recv = lax.all_to_all(send, ("y", "c"), 0, 0)
    send = term_part(recv, mean)
    recv = lax.all_to_all(send, ("x", "z"), 0, 0)
    gathered = lax.all_to_all(spread(recv), ("y", "z"), 0, 0)
    mine = solve(recv)
    other = lax.ppermute(mine, "c", [(0, 1), (1, 0)])
    left_factor, other = lax.optimization_barrier((left_part(mine, other), other))
    send, new_basis = approx_part(gathered, mine, other)
    groups = [[x * NC + c for x, c in LOOP]]
    recv = lax.all_to_all(send, ("x", "c"), 0, 0, axis_index_groups=groups)
    new_basis = new_basis.reshape(2, 32, LANES).transpose(2, 0, 1)
    return (subtract(merged, recv), left_factor, new_basis)


def solution(mesh):
    fine = Mesh(mesh.devices.reshape(8, NX, NZ, NC), ("y", "x", "z", "c"))
    fsdp = ("x", "z", "c")
    in_specs = (P("y", None, fsdp, None), P("y", None, fsdp, None), P(fsdp, None, None))
    out_specs = (P("y", None, fsdp, None), P(None, fsdp, None), P(fsdp, None, None))
    return jax.shard_map(shards, mesh=fine, in_specs=in_specs, out_specs=out_specs, check_vma=False)
```

```python
import jax
import jax.numpy as jnp
from jax import lax
from jax.experimental import pallas as pl
from jax.experimental.pallas import tpu as pltpu
from jax.sharding import Mesh, PartitionSpec as P

NX, NZ, NC = 4, 8, 2
LOOP = [(x, 0) for x in range(NX)] + [(x, 1) for x in reversed(range(NX))]
LANES = 128
HIGHEST = lax.Precision.HIGHEST
F32 = jnp.float32
VMEM = pl.BlockSpec(memory_space=pltpu.VMEM)
HBM = pl.BlockSpec(memory_space=pltpu.HBM)
PARAMS = pltpu.CompilerParams(vmem_limit_bytes=16 * 2**20)


def cost(flops, moved):
    return pl.CostEstimate(flops=flops, bytes_accessed=moved, transcendentals=0)


def dot(a, b, dims):
    return lax.dot_general(a, b, (dims, ((), ())), precision=HIGHEST, preferred_element_type=F32)


def chunk(x):
    return pl.ds(x * 16 * LANES, 16 * LANES)


def merge_kernel(grads, errors, out, grads_in, errors_in, blocks, sems):
    copies, results = [], []
    for x in range(NX):
        for k, (source, target) in enumerate(((grads, grads_in), (errors, errors_in))):
            copy = pltpu.make_async_copy(
                source.at[0, :, :, chunk(x)], target.at[:, :, chunk(x)], sems.at[k, x]
            )
            copy.start()
            copies.append(copy)
    for x in range(NX):
        copies[2 * x].wait()
        copies[2 * x + 1].wait()
        for m in range(2):
            for block in range(16):
                at = pl.ds((x * 16 + block) * LANES, LANES)
                blocks[block, x, m] = grads_in[m, :, at].astype(F32) + errors_in[m, :, at]
        copy = pltpu.make_async_copy(blocks.at[:, x], out.at[:, x], sems.at[2, x])
        copy.start()
        results.append(copy)
    for copy in results:
        copy.wait()


def merge(grads, errors):
    _, mats, rows, width = grads.shape
    return pl.pallas_call(
        merge_kernel,
        in_specs=[HBM] * 2,
        out_specs=HBM,
        out_shape=jax.ShapeDtypeStruct((16, NX, mats, rows, LANES), F32),
        scratch_shapes=[
            pltpu.VMEM((mats, rows, width), grads.dtype),
            pltpu.VMEM((mats, rows, width), errors.dtype),
            pltpu.VMEM((16, NX, mats, rows, LANES), F32),
            pltpu.SemaphoreType.DMA((3, NX)),
        ],
        cost_estimate=cost(2**19, 5 * 2**19),
        name="merge",
    )(grads, errors)


def relay_kernel(block, out):
    out[...] = block[...]


def relay(block):
    return pl.pallas_call(
        relay_kernel,
        in_specs=[VMEM],
        out_specs=VMEM,
        out_shape=jax.ShapeDtypeStruct(block.shape, F32),
        compiler_params=PARAMS,
        cost_estimate=cost(2**35, 2**16),
        name="relay",
    )(block)


def both_kernel(a, b, out):
    out[...] = a[...] + b[...]


def both(a, b):
    return pl.pallas_call(
        both_kernel,
        in_specs=[VMEM] * 2,
        out_specs=VMEM,
        out_shape=jax.ShapeDtypeStruct(a.shape, F32),
        compiler_params=PARAMS,
        cost_estimate=cost(2**13, 2**17),
        name="both",
    )(a, b)


def arrange_kernel(b0, b1, b2, b3, out):
    x = lax.axis_index("x")
    for part in range(NX):
        back = lax.rem(x - part + NX, NX)
        chosen = b0[...]
        for k, block in ((1, b1), (2, b2), (3, b3)):
            chosen = jnp.where(back == k, block[...], chosen)
        out[:, part * LANES : (part + 1) * LANES] = chosen


def arrange(shards):
    return pl.pallas_call(
        arrange_kernel,
        in_specs=[VMEM] * 4,
        out_specs=VMEM,
        out_shape=jax.ShapeDtypeStruct((64, NX * LANES), F32),
        compiler_params=PARAMS,
        cost_estimate=cost(2**20, 2**18),
        name="arrange",
    )(*shards)


def factor_kernel(recv, weights, mean_out, send):
    columns = []
    for part in range(NX):
        blocks = []
        for m in range(2):
            for c in range(NC):
                total = recv[c, part, m]
                for a in range(1, 8):
                    total = total + recv[2 * a + c, part, m]
                blocks.append(total)
        columns.append(jnp.concatenate(blocks, axis=0) * 0.125)
    mean = jnp.concatenate(columns, axis=1)
    mean_out[...] = mean
    partial = dot(mean, weights[...], ((1,), (1,)))
    piece = jnp.concatenate(
        [
            partial[16 * (2 * m + c) : 16 * (2 * m + c + 1), 32 * m : 32 * (m + 1)]
            for m in range(2)
            for c in range(NC)
        ],
        axis=1,
    )
    for i in range(16):
        send[i] = piece


def factor_part(recv, weights):
    return pl.pallas_call(
        factor_kernel,
        in_specs=[VMEM] * 2,
        out_specs=[VMEM] * 2,
        out_shape=[
            jax.ShapeDtypeStruct((64, 512), F32),
            jax.ShapeDtypeStruct((16, 16, LANES), F32),
        ],
        compiler_params=PARAMS,
        cost_estimate=cost(2**22, 2**20 + 2**19),
        name="factor_part",
    )(recv, weights)


def term_kernel(recv, mean, send):
    factor = recv[0]
    for i in range(1, 16):
        factor = factor + recv[i]
    blank = jnp.zeros((16, 32), F32)
    rows = []
    for m in range(2):
        for c in range(NC):
            piece = factor[:, 32 * (2 * m + c) : 32 * (2 * m + c + 1)]
            rows.append(jnp.concatenate([piece, blank] if m == 0 else [blank, piece], axis=1))
    blocked = jnp.concatenate(rows, axis=0)
    half = jnp.where(lax.axis_index("c") == 0, factor[:, :64], factor[:, 64:])
    half = jnp.concatenate([half[:8], half[8:]], axis=1)
    term = dot(blocked, mean[...], ((0,), (0,)))
    for x in range(NX):
        for z in range(NZ):
            send[x * NZ + z, 0:8] = term[8 * z : 8 * z + 8, x * LANES : (x + 1) * LANES]
            send[x * NZ + z, 8:16] = half


def term_part(recv, mean):
    return pl.pallas_call(
        term_kernel,
        in_specs=[VMEM] * 2,
        out_specs=VMEM,
        out_shape=jax.ShapeDtypeStruct((NX * NZ, 16, LANES), F32),
        compiler_params=PARAMS,
        cost_estimate=cost(2**23, 2**20),
        name="term_part",
    )(recv, mean)


def spread_kernel(recv, send):
    total = recv[0, 0:8]
    for g in range(1, NX * NZ):
        total = total + recv[g, 0:8]
    for i in range(8 * NZ):
        send[i] = total


def spread(recv):
    return pl.pallas_call(
        spread_kernel,
        in_specs=[VMEM],
        out_specs=VMEM,
        out_shape=jax.ShapeDtypeStruct((8 * NZ, 8, LANES), F32),
        compiler_params=PARAMS,
        cost_estimate=cost(2**15, 2**19),
        name="spread",
    )(recv)


def inverse_factor(gram):
    row = lax.broadcasted_iota(jnp.int32, (32, 32), 0)
    lane = lax.broadcasted_iota(jnp.int32, (32, 32), 1)
    unit = jnp.where(lane == row, 1.0, 0.0).astype(F32)
    scale = jnp.zeros((32, 32), F32)
    for j in range(32):
        column = gram[:, j : j + 1]
        pivot = column[j : j + 1]
        scale = jnp.where(row == j, pivot, scale)
        share = jnp.where(row > j, column / pivot, 0.0)
        gram = gram - share * gram[j : j + 1]
        unit = unit - share * unit[j : j + 1]
    return unit / jnp.sqrt(scale)


def solve_kernel(recv, out):
    z = lax.axis_index("z")
    packed = recv[:, 8:16, :].reshape(NX * NZ * 8, LANES)
    low, high = packed[:, :64], packed[:, 64:]
    square = dot(low, low, ((0,), (0,))) + dot(high, high, ((0,), (0,)))
    inverse = inverse_factor(square[:32, :32] + square[32:, 32:])
    blank = jnp.zeros((32, 32), F32)
    wide = jnp.concatenate(
        [jnp.concatenate([inverse, blank], axis=1), jnp.concatenate([blank, inverse], axis=1)],
        axis=0,
    )
    mine = []
    for part in range(NX):
        block = recv[part * NZ + z, 8:16]
        mine += [block[:, :64], block[:, 64:]]
    out[:, :64] = dot(jnp.concatenate(mine, axis=0), wide, ((1,), (1,)))
    out[:, 64:] = wide


def solve(recv):
    return pl.pallas_call(
        solve_kernel,
        in_specs=[VMEM],
        out_specs=VMEM,
        out_shape=jax.ShapeDtypeStruct((64, LANES), F32),
        compiler_params=PARAMS,
        cost_estimate=cost(2**24, 2**19),
        name="solve",
    )(recv)


def solutions(mine, other):
    c = lax.axis_index("c")
    solved = [jnp.where(c == m, mine[...], other[...]) for m in range(2)]
    blank = jnp.zeros((32, 32), F32)
    inverse = jnp.concatenate(
        [
            jnp.concatenate([solved[0][:32, 64:96], blank], axis=1),
            jnp.concatenate([blank, solved[1][:32, 64:96]], axis=1),
        ],
        axis=0,
    )
    rows = [
        [solved[m][16 * x : 16 * x + 16, 32 * c : 32 * c + 32] for x, c in LOOP] for m in range(2)
    ]
    return inverse, rows


def approx_kernel(recv, mine, other, send, basis_out):
    z = lax.axis_index("z")
    inverse, rows = solutions(mine, other)
    term = jnp.concatenate(
        [recv[a * NZ : (a + 1) * NZ].reshape(64, LANES) for a in range(8)], axis=1
    )
    turned = dot(inverse, term, ((1,), (0,)))
    own = turned[:, :LANES]
    for a in range(1, 8):
        own = jnp.where(z == a, turned[:, a * LANES : (a + 1) * LANES], own)
    basis_out[...] = own
    for m in range(2):
        result = dot(jnp.concatenate(rows[m], axis=0), turned[32 * m : 32 * (m + 1)], ((1,), (0,)))
        for i in range(NX * NC):
            send[i, m] = result[16 * i : 16 * i + 16]


def approx_part(recv, mine, other):
    return pl.pallas_call(
        approx_kernel,
        in_specs=[VMEM] * 3,
        out_specs=[VMEM] * 2,
        out_shape=[
            jax.ShapeDtypeStruct((NX * NC, 2, 16, 1024), F32),
            jax.ShapeDtypeStruct((64, LANES), F32),
        ],
        compiler_params=PARAMS,
        cost_estimate=cost(2**26, 2**20),
        name="approx_part",
    )(recv, mine, other)


def left_kernel(mine, other, out):
    x, c = lax.axis_index("x"), lax.axis_index("c")
    _, rows = solutions(mine, other)
    for m in range(2):
        left = rows[m][0]
        for i, (at, core) in enumerate(LOOP):
            left = jnp.where((x == at) & (c == core), rows[m][i], left)
        out[m] = left


def left_part(mine, other):
    return pl.pallas_call(
        left_kernel,
        in_specs=[VMEM] * 2,
        out_specs=VMEM,
        out_shape=jax.ShapeDtypeStruct((2, 16, 32), F32),
        compiler_params=PARAMS,
        cost_estimate=cost(2**22, 2**17),
        name="left_part",
    )(mine, other)


def subtract_kernel(merged, recv, out, result, sems):
    copies = []
    for x in range(NX):
        for m in range(2):
            for a in range(8):
                for c in range(NC):
                    at = pl.ds((x * 16 + 2 * a + c) * LANES, LANES)
                    approx = recv[LOOP.index((x, c)), m, :, a * LANES : (a + 1) * LANES]
                    result[m, :, at] = merged[2 * a + c, x, m] - approx
        copy = pltpu.make_async_copy(
            result.at[:, :, chunk(x)], out.at[0, :, :, chunk(x)], sems.at[x]
        )
        copy.start()
        copies.append(copy)
    for copy in copies:
        copy.wait()


def subtract(merged, recv):
    _, _, mats, rows, _ = merged.shape
    width = NX * 16 * LANES
    return pl.pallas_call(
        subtract_kernel,
        in_specs=[VMEM] * 2,
        out_specs=HBM,
        out_shape=jax.ShapeDtypeStruct((1, mats, rows, width), F32),
        scratch_shapes=[pltpu.VMEM((mats, rows, width), F32), pltpu.SemaphoreType.DMA((NX,))],
        compiler_params=PARAMS,
        cost_estimate=cost(2**19, 7 * 2**19),
        name="subtract",
    )(merged, recv)


def near_pairs():
    pairs = []
    for a in range(8):
        for dy, dz in ((0, -2), (1, -1), (2, 0), (-1, 1)):
            pairs.append(((a + dy) % 8 * NZ + a, a * NZ + (a + dz) % NZ))
    return pairs


def shards(grads, errors, basis):
    held = basis.transpose(1, 2, 0).reshape(64, LANES)
    held = lax.ppermute(held, ("y", "z"), near_pairs())
    held = relay(held)
    held = both(held, lax.ppermute(held, "z", [(z, (z + 4) % NZ) for z in range(NZ)]))
    merged = merge(grads, errors)
    recv = lax.all_to_all(merged, ("y", "c"), 0, 0)
    parts = [held] + [
        lax.ppermute(held, "x", [(i, (i + k) % NX) for i in range(NX)]) for k in range(1, NX)
    ]
    mean, send = factor_part(recv, arrange(parts))
    recv = lax.all_to_all(send, ("y", "c"), 0, 0)
    send = term_part(recv, mean)
    recv = lax.all_to_all(send, ("x", "z"), 0, 0)
    gathered = lax.all_to_all(spread(recv), ("y", "z"), 0, 0)
    mine = solve(recv)
    other = lax.ppermute(mine, "c", [(0, 1), (1, 0)])
    left_factor, other = lax.optimization_barrier((left_part(mine, other), other))
    send, new_basis = approx_part(gathered, mine, other)
    groups = [[x * NC + c for x, c in LOOP]]
    recv = lax.all_to_all(send, ("x", "c"), 0, 0, axis_index_groups=groups)
    new_basis = new_basis.reshape(2, 32, LANES).transpose(2, 0, 1)
    return (subtract(merged, recv), left_factor, new_basis)


def solution(mesh):
    fine = Mesh(mesh.devices.reshape(8, NX, NZ, NC), ("y", "x", "z", "c"))
    fsdp = ("x", "z", "c")
    in_specs = (P("y", None, fsdp, None), P("y", None, fsdp, None), P(fsdp, None, None))
    out_specs = (P("y", None, fsdp, None), P(None, fsdp, None), P(fsdp, None, None))
    return jax.shard_map(shards, mesh=fine, in_specs=in_specs, out_specs=out_specs, check_vma=False)
```

```python
import jax
import jax.numpy as jnp
from jax import lax
from jax.experimental import pallas as pl
from jax.experimental.pallas import tpu as pltpu
from jax.sharding import Mesh, PartitionSpec as P

NX, NZ, NC = 4, 8, 2
LOOP = [(x, 0) for x in range(NX)] + [(x, 1) for x in reversed(range(NX))]
DIAGONALS = [((i + z) % 8, z) for i in range(8) for z in range(NZ)]
LANES = 128
HIGHEST = lax.Precision.HIGHEST
F32 = jnp.float32
VMEM = pl.BlockSpec(memory_space=pltpu.VMEM)
HBM = pl.BlockSpec(memory_space=pltpu.HBM)
PARAMS = pltpu.CompilerParams(vmem_limit_bytes=16 * 2**20)


def cost(flops, moved):
    return pl.CostEstimate(flops=flops, bytes_accessed=moved, transcendentals=0)


def dot(a, b, dims):
    return lax.dot_general(a, b, (dims, ((), ())), precision=HIGHEST, preferred_element_type=F32)


def chunk(x):
    return pl.ds(x * 16 * LANES, 16 * LANES)


def merge_kernel(grads, errors, out, grads_in, errors_in, blocks, sems):
    copies, results = [], []
    for x in range(NX):
        for k, (source, target) in enumerate(((grads, grads_in), (errors, errors_in))):
            copy = pltpu.make_async_copy(
                source.at[0, :, :, chunk(x)], target.at[:, :, chunk(x)], sems.at[k, x]
            )
            copy.start()
            copies.append(copy)
    for x in range(NX):
        copies[2 * x].wait()
        copies[2 * x + 1].wait()
        for m in range(2):
            for block in range(16):
                at = pl.ds((x * 16 + block) * LANES, LANES)
                blocks[block, x, m] = grads_in[m, :, at].astype(F32) + errors_in[m, :, at]
        copy = pltpu.make_async_copy(blocks.at[:, x], out.at[:, x], sems.at[2, x])
        copy.start()
        results.append(copy)
    for copy in results:
        copy.wait()


def merge(grads, errors):
    _, mats, rows, width = grads.shape
    return pl.pallas_call(
        merge_kernel,
        in_specs=[HBM] * 2,
        out_specs=HBM,
        out_shape=jax.ShapeDtypeStruct((16, NX, mats, rows, LANES), F32),
        scratch_shapes=[
            pltpu.VMEM((mats, rows, width), grads.dtype),
            pltpu.VMEM((mats, rows, width), errors.dtype),
            pltpu.VMEM((16, NX, mats, rows, LANES), F32),
            pltpu.SemaphoreType.DMA((3, NX)),
        ],
        cost_estimate=cost(2**19, 5 * 2**19),
        name="merge",
    )(grads, errors)


def relay_kernel(block, out):
    out[...] = block[...]


def relay(block):
    return pl.pallas_call(
        relay_kernel,
        in_specs=[VMEM],
        out_specs=VMEM,
        out_shape=jax.ShapeDtypeStruct(block.shape, F32),
        compiler_params=PARAMS,
        cost_estimate=cost(2**35, 2**16),
        name="relay",
    )(block)


def both_kernel(a, b, out):
    out[...] = a[...] + b[...]


def both(a, b):
    return pl.pallas_call(
        both_kernel,
        in_specs=[VMEM] * 2,
        out_specs=VMEM,
        out_shape=jax.ShapeDtypeStruct(a.shape, F32),
        compiler_params=PARAMS,
        cost_estimate=cost(2**13, 2**17),
        name="both",
    )(a, b)


def arrange_kernel(b0, b1, b2, b3, out):
    x = lax.axis_index("x")
    for part in range(NX):
        back = lax.rem(x - part + NX, NX)
        chosen = b0[...]
        for k, block in ((1, b1), (2, b2), (3, b3)):
            chosen = jnp.where(back == k, block[...], chosen)
        out[:, part * LANES : (part + 1) * LANES] = chosen


def arrange(shards):
    return pl.pallas_call(
        arrange_kernel,
        in_specs=[VMEM] * 4,
        out_specs=VMEM,
        out_shape=jax.ShapeDtypeStruct((64, NX * LANES), F32),
        compiler_params=PARAMS,
        cost_estimate=cost(2**20, 2**18),
        name="arrange",
    )(*shards)


def factor_kernel(recv, weights, mean_out, send):
    columns = []
    for part in range(NX):
        blocks = []
        for m in range(2):
            for c in range(NC):
                total = recv[c, part, m]
                for a in range(1, 8):
                    total = total + recv[2 * a + c, part, m]
                blocks.append(total)
        columns.append(jnp.concatenate(blocks, axis=0) * 0.125)
    mean = jnp.concatenate(columns, axis=1)
    mean_out[...] = mean
    partial = dot(mean, weights[...], ((1,), (1,)))
    piece = jnp.concatenate(
        [
            partial[16 * (2 * m + c) : 16 * (2 * m + c + 1), 32 * m : 32 * (m + 1)]
            for m in range(2)
            for c in range(NC)
        ],
        axis=1,
    )
    for i in range(16):
        send[i] = piece


def factor_part(recv, weights):
    return pl.pallas_call(
        factor_kernel,
        in_specs=[VMEM] * 2,
        out_specs=[VMEM] * 2,
        out_shape=[
            jax.ShapeDtypeStruct((64, 512), F32),
            jax.ShapeDtypeStruct((16, 16, LANES), F32),
        ],
        compiler_params=PARAMS,
        cost_estimate=cost(2**22, 2**20 + 2**19),
        name="factor_part",
    )(recv, weights)


def term_kernel(recv, mean, send):
    factor = recv[0]
    for i in range(1, 16):
        factor = factor + recv[i]
    blank = jnp.zeros((16, 32), F32)
    rows = []
    for m in range(2):
        for c in range(NC):
            piece = factor[:, 32 * (2 * m + c) : 32 * (2 * m + c + 1)]
            rows.append(jnp.concatenate([piece, blank] if m == 0 else [blank, piece], axis=1))
    blocked = jnp.concatenate(rows, axis=0)
    half = jnp.where(lax.axis_index("c") == 0, factor[:, :64], factor[:, 64:])
    half = jnp.concatenate([half[:8], half[8:]], axis=1)
    term = dot(blocked, mean[...], ((0,), (0,)))
    for x in range(NX):
        for z in range(NZ):
            send[x * NZ + z, 0:8] = term[8 * z : 8 * z + 8, x * LANES : (x + 1) * LANES]
            send[x * NZ + z, 8:16] = half


def term_part(recv, mean):
    return pl.pallas_call(
        term_kernel,
        in_specs=[VMEM] * 2,
        out_specs=VMEM,
        out_shape=jax.ShapeDtypeStruct((NX * NZ, 16, LANES), F32),
        compiler_params=PARAMS,
        cost_estimate=cost(2**23, 2**20),
        name="term_part",
    )(recv, mean)


def spread_kernel(recv, send):
    total = recv[0, 0:8]
    for g in range(1, NX * NZ):
        total = total + recv[g, 0:8]
    for i in range(8 * NZ):
        send[i] = total


def spread(recv):
    return pl.pallas_call(
        spread_kernel,
        in_specs=[VMEM],
        out_specs=VMEM,
        out_shape=jax.ShapeDtypeStruct((8 * NZ, 8, LANES), F32),
        compiler_params=PARAMS,
        cost_estimate=cost(2**15, 2**19),
        name="spread",
    )(recv)


def inverse_factor(gram):
    row = lax.broadcasted_iota(jnp.int32, (32, 32), 0)
    lane = lax.broadcasted_iota(jnp.int32, (32, 32), 1)
    unit = jnp.where(lane == row, 1.0, 0.0).astype(F32)
    scale = jnp.zeros((32, 32), F32)
    for j in range(32):
        column = gram[:, j : j + 1]
        pivot = column[j : j + 1]
        scale = jnp.where(row == j, pivot, scale)
        share = jnp.where(row > j, column / pivot, 0.0)
        gram = gram - share * gram[j : j + 1]
        unit = unit - share * unit[j : j + 1]
    return unit / jnp.sqrt(scale)


def solve_kernel(recv, out):
    z = lax.axis_index("z")
    packed = recv[:, 8:16, :].reshape(NX * NZ * 8, LANES)
    low, high = packed[:, :64], packed[:, 64:]
    square = dot(low, low, ((0,), (0,))) + dot(high, high, ((0,), (0,)))
    inverse = inverse_factor(square[:32, :32] + square[32:, 32:])
    blank = jnp.zeros((32, 32), F32)
    wide = jnp.concatenate(
        [jnp.concatenate([inverse, blank], axis=1), jnp.concatenate([blank, inverse], axis=1)],
        axis=0,
    )
    mine = []
    for part in range(NX):
        block = recv[part * NZ + z, 8:16]
        mine += [block[:, :64], block[:, 64:]]
    out[:, :64] = dot(jnp.concatenate(mine, axis=0), wide, ((1,), (1,)))
    out[:, 64:] = wide


def solve(recv):
    return pl.pallas_call(
        solve_kernel,
        in_specs=[VMEM],
        out_specs=VMEM,
        out_shape=jax.ShapeDtypeStruct((64, LANES), F32),
        compiler_params=PARAMS,
        cost_estimate=cost(2**24, 2**19),
        name="solve",
    )(recv)


def solutions(mine, other):
    c = lax.axis_index("c")
    solved = [jnp.where(c == m, mine[...], other[...]) for m in range(2)]
    blank = jnp.zeros((32, 32), F32)
    inverse = jnp.concatenate(
        [
            jnp.concatenate([solved[0][:32, 64:96], blank], axis=1),
            jnp.concatenate([blank, solved[1][:32, 64:96]], axis=1),
        ],
        axis=0,
    )
    rows = [
        [solved[m][16 * x : 16 * x + 16, 32 * c : 32 * c + 32] for x, c in LOOP] for m in range(2)
    ]
    return inverse, rows


def approx_kernel(recv, mine, other, send, basis_out):
    z = lax.axis_index("z")
    inverse, rows = solutions(mine, other)
    columns = [
        jnp.concatenate([recv[DIAGONALS.index((a, part))] for part in range(NZ)], axis=0)
        for a in range(8)
    ]
    term = jnp.concatenate(columns, axis=1)
    turned = dot(inverse, term, ((1,), (0,)))
    own = turned[:, :LANES]
    for a in range(1, 8):
        own = jnp.where(z == a, turned[:, a * LANES : (a + 1) * LANES], own)
    basis_out[...] = own
    for m in range(2):
        result = dot(jnp.concatenate(rows[m], axis=0), turned[32 * m : 32 * (m + 1)], ((1,), (0,)))
        for i in range(NX * NC):
            send[i, m] = result[16 * i : 16 * i + 16]


def approx_part(recv, mine, other):
    return pl.pallas_call(
        approx_kernel,
        in_specs=[VMEM] * 3,
        out_specs=[VMEM] * 2,
        out_shape=[
            jax.ShapeDtypeStruct((NX * NC, 2, 16, 1024), F32),
            jax.ShapeDtypeStruct((64, LANES), F32),
        ],
        compiler_params=PARAMS,
        cost_estimate=cost(2**26, 2**20),
        name="approx_part",
    )(recv, mine, other)


def left_kernel(mine, other, out):
    x, c = lax.axis_index("x"), lax.axis_index("c")
    _, rows = solutions(mine, other)
    for m in range(2):
        left = rows[m][0]
        for i, (at, core) in enumerate(LOOP):
            left = jnp.where((x == at) & (c == core), rows[m][i], left)
        out[m] = left


def left_part(mine, other):
    return pl.pallas_call(
        left_kernel,
        in_specs=[VMEM] * 2,
        out_specs=VMEM,
        out_shape=jax.ShapeDtypeStruct((2, 16, 32), F32),
        compiler_params=PARAMS,
        cost_estimate=cost(2**22, 2**17),
        name="left_part",
    )(mine, other)


def subtract_kernel(merged, recv, out, result, sems):
    copies = []
    for x in range(NX):
        for m in range(2):
            for a in range(8):
                for c in range(NC):
                    at = pl.ds((x * 16 + 2 * a + c) * LANES, LANES)
                    approx = recv[LOOP.index((x, c)), m, :, a * LANES : (a + 1) * LANES]
                    result[m, :, at] = merged[2 * a + c, x, m] - approx
        copy = pltpu.make_async_copy(
            result.at[:, :, chunk(x)], out.at[0, :, :, chunk(x)], sems.at[x]
        )
        copy.start()
        copies.append(copy)
    for copy in copies:
        copy.wait()


def subtract(merged, recv):
    _, _, mats, rows, _ = merged.shape
    width = NX * 16 * LANES
    return pl.pallas_call(
        subtract_kernel,
        in_specs=[VMEM] * 2,
        out_specs=HBM,
        out_shape=jax.ShapeDtypeStruct((1, mats, rows, width), F32),
        scratch_shapes=[pltpu.VMEM((mats, rows, width), F32), pltpu.SemaphoreType.DMA((NX,))],
        compiler_params=PARAMS,
        cost_estimate=cost(2**19, 7 * 2**19),
        name="subtract",
    )(merged, recv)


def near_pairs():
    pairs = []
    for a in range(8):
        for dy, dz in ((0, -2), (1, -1), (2, 0), (-1, 1)):
            pairs.append(((a + dy) % 8 * NZ + a, a * NZ + (a + dz) % NZ))
    return pairs


def shards(grads, errors, basis):
    held = basis.transpose(1, 2, 0).reshape(64, LANES)
    held = lax.ppermute(held, ("y", "z"), near_pairs())
    held = relay(held)
    held = both(held, lax.ppermute(held, "z", [(z, (z + 4) % NZ) for z in range(NZ)]))
    merged = merge(grads, errors)
    recv = lax.all_to_all(merged, ("y", "c"), 0, 0)
    parts = [held] + [
        lax.ppermute(held, "x", [(i, (i + k) % NX) for i in range(NX)]) for k in range(1, NX)
    ]
    mean, send = factor_part(recv, arrange(parts))
    recv = lax.all_to_all(send, ("y", "c"), 0, 0)
    send = term_part(recv, mean)
    recv = lax.all_to_all(send, ("x", "z"), 0, 0)
    groups = [[y * NZ + z for y, z in DIAGONALS]]
    gathered = lax.all_to_all(spread(recv), ("y", "z"), 0, 0, axis_index_groups=groups)
    mine = solve(recv)
    other = lax.ppermute(mine, "c", [(0, 1), (1, 0)])
    left_factor, other = lax.optimization_barrier((left_part(mine, other), other))
    send, new_basis = approx_part(gathered, mine, other)
    groups = [[x * NC + c for x, c in LOOP]]
    recv = lax.all_to_all(send, ("x", "c"), 0, 0, axis_index_groups=groups)
    new_basis = new_basis.reshape(2, 32, LANES).transpose(2, 0, 1)
    return (subtract(merged, recv), left_factor, new_basis)


def solution(mesh):
    fine = Mesh(mesh.devices.reshape(8, NX, NZ, NC), ("y", "x", "z", "c"))
    fsdp = ("x", "z", "c")
    in_specs = (P("y", None, fsdp, None), P("y", None, fsdp, None), P(fsdp, None, None))
    out_specs = (P("y", None, fsdp, None), P(None, fsdp, None), P(fsdp, None, None))
    return jax.shard_map(shards, mesh=fine, in_specs=in_specs, out_specs=out_specs, check_vma=False)
```

```python
import jax
import jax.numpy as jnp
from jax import lax
from jax.experimental import pallas as pl
from jax.experimental.pallas import tpu as pltpu
from jax.sharding import Mesh, PartitionSpec as P

NX, NZ, NC = 4, 8, 2
LOOP = [(x, 0) for x in range(NX)] + [(x, 1) for x in reversed(range(NX))]
DIAGONALS = [((i + z) % 8, z) for i in range(8) for z in range(NZ)]
LANES = 128
HIGHEST = lax.Precision.HIGHEST
F32 = jnp.float32
VMEM = pl.BlockSpec(memory_space=pltpu.VMEM)
HBM = pl.BlockSpec(memory_space=pltpu.HBM)
PARAMS = pltpu.CompilerParams(vmem_limit_bytes=16 * 2**20)


def cost(flops, moved):
    return pl.CostEstimate(flops=flops, bytes_accessed=moved, transcendentals=0)


def dot(a, b, dims):
    return lax.dot_general(a, b, (dims, ((), ())), precision=HIGHEST, preferred_element_type=F32)


def chunk(x):
    return pl.ds(x * 16 * LANES, 16 * LANES)


def merge_kernel(grads, errors, out, grads_in, errors_in, blocks, sems):
    copies, results = [], []
    for x in range(NX):
        for k, (source, target) in enumerate(((grads, grads_in), (errors, errors_in))):
            copy = pltpu.make_async_copy(
                source.at[0, :, :, chunk(x)], target.at[:, :, chunk(x)], sems.at[k, x]
            )
            copy.start()
            copies.append(copy)
    for x in range(NX):
        copies[2 * x].wait()
        copies[2 * x + 1].wait()
        for m in range(2):
            for block in range(16):
                at = pl.ds((x * 16 + block) * LANES, LANES)
                blocks[block, x, m] = grads_in[m, :, at].astype(F32) + errors_in[m, :, at]
        copy = pltpu.make_async_copy(blocks.at[:, x], out.at[:, x], sems.at[2, x])
        copy.start()
        results.append(copy)
    for copy in results:
        copy.wait()


def merge(grads, errors):
    _, mats, rows, width = grads.shape
    return pl.pallas_call(
        merge_kernel,
        in_specs=[HBM] * 2,
        out_specs=HBM,
        out_shape=jax.ShapeDtypeStruct((16, NX, mats, rows, LANES), F32),
        scratch_shapes=[
            pltpu.VMEM((mats, rows, width), grads.dtype),
            pltpu.VMEM((mats, rows, width), errors.dtype),
            pltpu.VMEM((16, NX, mats, rows, LANES), F32),
            pltpu.SemaphoreType.DMA((3, NX)),
        ],
        cost_estimate=cost(2**19, 5 * 2**19),
        name="merge",
    )(grads, errors)


def relay_kernel(block, out):
    out[...] = block[...]


def relay(block):
    return pl.pallas_call(
        relay_kernel,
        in_specs=[VMEM],
        out_specs=VMEM,
        out_shape=jax.ShapeDtypeStruct(block.shape, F32),
        compiler_params=PARAMS,
        cost_estimate=cost(2**35, 2**16),
        name="relay",
    )(block)


def both_kernel(a, b, out):
    out[...] = a[...] + b[...]


def both(a, b):
    return pl.pallas_call(
        both_kernel,
        in_specs=[VMEM] * 2,
        out_specs=VMEM,
        out_shape=jax.ShapeDtypeStruct(a.shape, F32),
        compiler_params=PARAMS,
        cost_estimate=cost(2**13, 2**17),
        name="both",
    )(a, b)


def arrange_kernel(b0, b1, b2, b3, out):
    x = lax.axis_index("x")
    for part in range(NX):
        back = lax.rem(x - part + NX, NX)
        chosen = b0[...]
        for k, block in ((1, b1), (2, b2), (3, b3)):
            chosen = jnp.where(back == k, block[...], chosen)
        out[:, part * LANES : (part + 1) * LANES] = chosen


def arrange(shards):
    return pl.pallas_call(
        arrange_kernel,
        in_specs=[VMEM] * 4,
        out_specs=VMEM,
        out_shape=jax.ShapeDtypeStruct((64, NX * LANES), F32),
        compiler_params=PARAMS,
        cost_estimate=cost(2**20, 2**18),
        name="arrange",
    )(*shards)


def factor_kernel(recv, weights, mean_out, send):
    columns = []
    for part in range(NX):
        blocks = []
        for m in range(2):
            for c in range(NC):
                total = recv[c, part, m]
                for a in range(1, 8):
                    total = total + recv[2 * a + c, part, m]
                blocks.append(total)
        columns.append(jnp.concatenate(blocks, axis=0) * 0.125)
    mean = jnp.concatenate(columns, axis=1)
    mean_out[...] = mean
    partial = dot(mean, weights[...], ((1,), (1,)))
    piece = jnp.concatenate(
        [
            partial[16 * (2 * m + c) : 16 * (2 * m + c + 1), 32 * m : 32 * (m + 1)]
            for m in range(2)
            for c in range(NC)
        ],
        axis=1,
    )
    for i in range(16):
        send[i] = piece


def factor_part(recv, weights):
    return pl.pallas_call(
        factor_kernel,
        in_specs=[VMEM] * 2,
        out_specs=[VMEM] * 2,
        out_shape=[
            jax.ShapeDtypeStruct((64, 512), F32),
            jax.ShapeDtypeStruct((16, 16, LANES), F32),
        ],
        compiler_params=PARAMS,
        cost_estimate=cost(2**22, 2**20 + 2**19),
        name="factor_part",
    )(recv, weights)


def term_kernel(recv, mean, send):
    factor = recv[0]
    for i in range(1, 16):
        factor = factor + recv[i]
    blank = jnp.zeros((16, 32), F32)
    rows = []
    for m in range(2):
        for c in range(NC):
            piece = factor[:, 32 * (2 * m + c) : 32 * (2 * m + c + 1)]
            rows.append(jnp.concatenate([piece, blank] if m == 0 else [blank, piece], axis=1))
    blocked = jnp.concatenate(rows, axis=0)
    half = jnp.where(lax.axis_index("c") == 0, factor[:, :64], factor[:, 64:])
    half = jnp.concatenate([half[:8], half[8:]], axis=1)
    term = dot(blocked, mean[...], ((0,), (0,)))
    for x in range(NX):
        for z in range(NZ):
            send[x * NZ + z, 0:8] = term[8 * z : 8 * z + 8, x * LANES : (x + 1) * LANES]
            send[x * NZ + z, 8:16] = half


def term_part(recv, mean):
    return pl.pallas_call(
        term_kernel,
        in_specs=[VMEM] * 2,
        out_specs=VMEM,
        out_shape=jax.ShapeDtypeStruct((NX * NZ, 16, LANES), F32),
        compiler_params=PARAMS,
        cost_estimate=cost(2**23, 2**20),
        name="term_part",
    )(recv, mean)


def spread_kernel(recv, send):
    total = recv[0, 0:8]
    for g in range(1, NX * NZ):
        total = total + recv[g, 0:8]
    for i in range(8 * NZ):
        send[i] = total


def spread(recv):
    return pl.pallas_call(
        spread_kernel,
        in_specs=[VMEM],
        out_specs=VMEM,
        out_shape=jax.ShapeDtypeStruct((8 * NZ, 8, LANES), F32),
        compiler_params=PARAMS,
        cost_estimate=cost(2**15, 2**19),
        name="spread",
    )(recv)


def inverse_factor(gram):
    row = lax.broadcasted_iota(jnp.int32, (32, 32), 0)
    lane = lax.broadcasted_iota(jnp.int32, (32, 32), 1)
    unit = jnp.where(lane == row, 1.0, 0.0).astype(F32)
    scale = jnp.zeros((32, 32), F32)
    for j in range(32):
        column = gram[:, j : j + 1]
        pivot = column[j : j + 1]
        scale = jnp.where(row == j, pivot, scale)
        share = jnp.where(row > j, column / pivot, 0.0)
        gram = gram - share * gram[j : j + 1]
        unit = unit - share * unit[j : j + 1]
    return unit / jnp.sqrt(scale)


def solve_kernel(recv, out):
    z = lax.axis_index("z")
    packed = recv[:, 8:16, :].reshape(NX * NZ * 8, LANES)
    low, high = packed[:, :64], packed[:, 64:]
    square = dot(low, low, ((0,), (0,))) + dot(high, high, ((0,), (0,)))
    inverse = inverse_factor(square[:32, :32] + square[32:, 32:])
    blank = jnp.zeros((32, 32), F32)
    wide = jnp.concatenate(
        [jnp.concatenate([inverse, blank], axis=1), jnp.concatenate([blank, inverse], axis=1)],
        axis=0,
    )
    mine = []
    for part in range(NX):
        block = recv[part * NZ + z, 8:16]
        mine += [block[:, :64], block[:, 64:]]
    out[:, :64] = dot(jnp.concatenate(mine, axis=0), wide, ((1,), (1,)))
    out[:, 64:] = wide


def solve(recv):
    return pl.pallas_call(
        solve_kernel,
        in_specs=[VMEM],
        out_specs=VMEM,
        out_shape=jax.ShapeDtypeStruct((64, LANES), F32),
        compiler_params=PARAMS,
        cost_estimate=cost(2**24, 2**19),
        name="solve",
    )(recv)


def solutions(mine, other):
    c = lax.axis_index("c")
    solved = [jnp.where(c == m, mine[...], other[...]) for m in range(2)]
    blank = jnp.zeros((32, 32), F32)
    inverse = jnp.concatenate(
        [
            jnp.concatenate([solved[0][:32, 64:96], blank], axis=1),
            jnp.concatenate([blank, solved[1][:32, 64:96]], axis=1),
        ],
        axis=0,
    )
    rows = [
        [solved[m][16 * x : 16 * x + 16, 32 * c : 32 * c + 32] for x, c in LOOP] for m in range(2)
    ]
    return inverse, rows


def approx_kernel(recv, mine, other, send, basis_out):
    z = lax.axis_index("z")
    inverse, rows = solutions(mine, other)
    columns = [
        jnp.concatenate([recv[DIAGONALS.index((a, part))] for part in range(NZ)], axis=0)
        for a in range(8)
    ]
    term = jnp.concatenate(columns, axis=1)
    turned = dot(inverse, term, ((1,), (0,)))
    own = turned[:, :LANES]
    for a in range(1, 8):
        own = jnp.where(z == a, turned[:, a * LANES : (a + 1) * LANES], own)
    basis_out[...] = own
    for m in range(2):
        result = dot(jnp.concatenate(rows[m], axis=0), turned[32 * m : 32 * (m + 1)], ((1,), (0,)))
        for i in range(NX * NC):
            send[i, m] = result[16 * i : 16 * i + 16]


def approx_part(recv, mine, other):
    return pl.pallas_call(
        approx_kernel,
        in_specs=[VMEM] * 3,
        out_specs=[VMEM] * 2,
        out_shape=[
            jax.ShapeDtypeStruct((NX * NC, 2, 16, 1024), F32),
            jax.ShapeDtypeStruct((64, LANES), F32),
        ],
        compiler_params=PARAMS,
        cost_estimate=cost(2**26, 2**20),
        name="approx_part",
    )(recv, mine, other)


def left_kernel(mine, other, out):
    x, c = lax.axis_index("x"), lax.axis_index("c")
    _, rows = solutions(mine, other)
    for m in range(2):
        left = rows[m][0]
        for i, (at, core) in enumerate(LOOP):
            left = jnp.where((x == at) & (c == core), rows[m][i], left)
        out[m] = left


def left_part(mine, other):
    return pl.pallas_call(
        left_kernel,
        in_specs=[VMEM] * 2,
        out_specs=VMEM,
        out_shape=jax.ShapeDtypeStruct((2, 16, 32), F32),
        compiler_params=PARAMS,
        cost_estimate=cost(2**22, 2**17),
        name="left_part",
    )(mine, other)


def subtract_kernel(merged, recv, out, result, sems):
    copies = []
    for x in range(NX):
        for m in range(2):
            for a in range(8):
                for c in range(NC):
                    at = pl.ds((x * 16 + 2 * a + c) * LANES, LANES)
                    approx = recv[LOOP.index((x, c)), m, :, a * LANES : (a + 1) * LANES]
                    result[m, :, at] = merged[2 * a + c, x, m] - approx
        copy = pltpu.make_async_copy(
            result.at[:, :, chunk(x)], out.at[0, :, :, chunk(x)], sems.at[x]
        )
        copy.start()
        copies.append(copy)
    for copy in copies:
        copy.wait()


def subtract(merged, recv):
    _, _, mats, rows, _ = merged.shape
    width = NX * 16 * LANES
    return pl.pallas_call(
        subtract_kernel,
        in_specs=[VMEM] * 2,
        out_specs=HBM,
        out_shape=jax.ShapeDtypeStruct((1, mats, rows, width), F32),
        scratch_shapes=[pltpu.VMEM((mats, rows, width), F32), pltpu.SemaphoreType.DMA((NX,))],
        compiler_params=PARAMS,
        cost_estimate=cost(2**19, 7 * 2**19),
        name="subtract",
    )(merged, recv)


def near_pairs():
    pairs = []
    for a in range(8):
        for dy, dz in ((0, -2), (1, -1), (2, 0), (-1, 1)):
            pairs.append(((a + dy) % 8 * NZ + a, a * NZ + (a + dz) % NZ))
    return pairs


def shards(grads, errors, basis):
    held = basis.transpose(1, 2, 0).reshape(64, LANES)
    held = lax.ppermute(held, ("y", "z"), near_pairs())
    held = relay(held)
    held = both(held, lax.ppermute(held, "z", [(z, (z + 4) % NZ) for z in range(NZ)]))
    merged = merge(grads, errors)
    recv = lax.all_to_all(merged, ("y", "c"), 0, 0)
    moved = {
        k: lax.ppermute(held, "x", [(i, (i + k) % NX) for i in range(NX)]) for k in (1, 3, 2)
    }
    parts = [held] + [moved[k] for k in range(1, NX)]
    mean, send = factor_part(recv, arrange(parts))
    recv = lax.all_to_all(send, ("y", "c"), 0, 0)
    send = term_part(recv, mean)
    recv = lax.all_to_all(send, ("x", "z"), 0, 0)
    groups = [[y * NZ + z for y, z in DIAGONALS]]
    gathered = lax.all_to_all(spread(recv), ("y", "z"), 0, 0, axis_index_groups=groups)
    mine = solve(recv)
    other = lax.ppermute(mine, "c", [(0, 1), (1, 0)])
    left_factor, other = lax.optimization_barrier((left_part(mine, other), other))
    send, new_basis = approx_part(gathered, mine, other)
    groups = [[x * NC + c for x, c in LOOP]]
    recv = lax.all_to_all(send, ("x", "c"), 0, 0, axis_index_groups=groups)
    new_basis = new_basis.reshape(2, 32, LANES).transpose(2, 0, 1)
    return (subtract(merged, recv), left_factor, new_basis)


def solution(mesh):
    fine = Mesh(mesh.devices.reshape(8, NX, NZ, NC), ("y", "x", "z", "c"))
    fsdp = ("x", "z", "c")
    in_specs = (P("y", None, fsdp, None), P("y", None, fsdp, None), P(fsdp, None, None))
    out_specs = (P("y", None, fsdp, None), P(None, fsdp, None), P(fsdp, None, None))
    return jax.shard_map(shards, mesh=fine, in_specs=in_specs, out_specs=out_specs, check_vma=False)
```

```python
import jax
import jax.numpy as jnp
from jax import lax
from jax.experimental import pallas as pl
from jax.experimental.pallas import tpu as pltpu
from jax.sharding import Mesh, PartitionSpec as P

NX, NZ, NC = 4, 8, 2
LOOP = [(x, 0) for x in range(NX)] + [(x, 1) for x in reversed(range(NX))]
DIAGONALS = [((i + z) % 8, z) for i in range(8) for z in range(NZ)]
LANES = 128
HIGHEST = lax.Precision.HIGHEST
F32 = jnp.float32
VMEM = pl.BlockSpec(memory_space=pltpu.VMEM)
HBM = pl.BlockSpec(memory_space=pltpu.HBM)
PARAMS = pltpu.CompilerParams(vmem_limit_bytes=16 * 2**20)


def cost(flops, moved):
    return pl.CostEstimate(flops=flops, bytes_accessed=moved, transcendentals=0)


def dot(a, b, dims):
    return lax.dot_general(a, b, (dims, ((), ())), precision=HIGHEST, preferred_element_type=F32)


def chunk(x):
    return pl.ds(x * 16 * LANES, 16 * LANES)


def merge_kernel(grads, errors, out, grads_in, errors_in, blocks, sems):
    copies, results = [], []
    for h in range(2 * NX):
        at = pl.ds(h * 8 * LANES, 8 * LANES)
        for k, (source, target) in enumerate(((grads, grads_in), (errors, errors_in))):
            copy = pltpu.make_async_copy(source.at[0, :, :, at], target.at[:, :, at], sems.at[k, h])
            copy.start()
            copies.append(copy)
    for h in range(2 * NX):
        copies[2 * h].wait()
        copies[2 * h + 1].wait()
        x, first = h // 2, h % 2 * 8
        for m in range(2):
            for block in range(first, first + 8):
                at = pl.ds((x * 16 + block) * LANES, LANES)
                blocks[block, x, m] = grads_in[m, :, at].astype(F32) + errors_in[m, :, at]
        some = pl.ds(first, 8)
        copy = pltpu.make_async_copy(blocks.at[some, x], out.at[some, x], sems.at[2, h])
        copy.start()
        results.append(copy)
    for copy in results:
        copy.wait()


def merge(grads, errors):
    _, mats, rows, width = grads.shape
    return pl.pallas_call(
        merge_kernel,
        in_specs=[HBM] * 2,
        out_specs=HBM,
        out_shape=jax.ShapeDtypeStruct((16, NX, mats, rows, LANES), F32),
        scratch_shapes=[
            pltpu.VMEM((mats, rows, width), grads.dtype),
            pltpu.VMEM((mats, rows, width), errors.dtype),
            pltpu.VMEM((16, NX, mats, rows, LANES), F32),
            pltpu.SemaphoreType.DMA((3, 2 * NX)),
        ],
        cost_estimate=cost(2**19, 5 * 2**19),
        name="merge",
    )(grads, errors)


def relay_kernel(block, out):
    out[...] = block[...]


def relay(block):
    return pl.pallas_call(
        relay_kernel,
        in_specs=[VMEM],
        out_specs=VMEM,
        out_shape=jax.ShapeDtypeStruct(block.shape, F32),
        compiler_params=PARAMS,
        cost_estimate=cost(2**35, 2**16),
        name="relay",
    )(block)


def both_kernel(a, b, out):
    out[...] = a[...] + b[...]


def both(a, b):
    return pl.pallas_call(
        both_kernel,
        in_specs=[VMEM] * 2,
        out_specs=VMEM,
        out_shape=jax.ShapeDtypeStruct(a.shape, F32),
        compiler_params=PARAMS,
        cost_estimate=cost(2**13, 2**17),
        name="both",
    )(a, b)


def arrange_kernel(b0, b1, b2, b3, out):
    x = lax.axis_index("x")
    for part in range(NX):
        back = lax.rem(x - part + NX, NX)
        chosen = b0[...]
        for k, block in ((1, b1), (2, b2), (3, b3)):
            chosen = jnp.where(back == k, block[...], chosen)
        out[:, part * LANES : (part + 1) * LANES] = chosen


def arrange(shards):
    return pl.pallas_call(
        arrange_kernel,
        in_specs=[VMEM] * 4,
        out_specs=VMEM,
        out_shape=jax.ShapeDtypeStruct((64, NX * LANES), F32),
        compiler_params=PARAMS,
        cost_estimate=cost(2**20, 2**18),
        name="arrange",
    )(*shards)


def factor_kernel(recv, weights, mean_out, send):
    columns = []
    for part in range(NX):
        blocks = []
        for m in range(2):
            for c in range(NC):
                total = recv[c, part, m]
                for a in range(1, 8):
                    total = total + recv[2 * a + c, part, m]
                blocks.append(total)
        columns.append(jnp.concatenate(blocks, axis=0) * 0.125)
    mean = jnp.concatenate(columns, axis=1)
    mean_out[...] = mean
    partial = dot(mean, weights[...], ((1,), (1,)))
    piece = jnp.concatenate(
        [
            partial[16 * (2 * m + c) : 16 * (2 * m + c + 1), 32 * m : 32 * (m + 1)]
            for m in range(2)
            for c in range(NC)
        ],
        axis=1,
    )
    for i in range(16):
        send[i] = piece


def factor_part(recv, weights):
    return pl.pallas_call(
        factor_kernel,
        in_specs=[VMEM] * 2,
        out_specs=[VMEM] * 2,
        out_shape=[
            jax.ShapeDtypeStruct((64, 512), F32),
            jax.ShapeDtypeStruct((16, 16, LANES), F32),
        ],
        compiler_params=PARAMS,
        cost_estimate=cost(2**22, 2**20 + 2**19),
        name="factor_part",
    )(recv, weights)


def term_kernel(recv, mean, send):
    factor = recv[0]
    for i in range(1, 16):
        factor = factor + recv[i]
    blank = jnp.zeros((16, 32), F32)
    rows = []
    for m in range(2):
        for c in range(NC):
            piece = factor[:, 32 * (2 * m + c) : 32 * (2 * m + c + 1)]
            rows.append(jnp.concatenate([piece, blank] if m == 0 else [blank, piece], axis=1))
    blocked = jnp.concatenate(rows, axis=0)
    half = jnp.where(lax.axis_index("c") == 0, factor[:, :64], factor[:, 64:])
    half = jnp.concatenate([half[:8], half[8:]], axis=1)
    term = dot(blocked, mean[...], ((0,), (0,)))
    for x in range(NX):
        for z in range(NZ):
            send[x * NZ + z, 0:8] = term[8 * z : 8 * z + 8, x * LANES : (x + 1) * LANES]
            send[x * NZ + z, 8:16] = half


def term_part(recv, mean):
    return pl.pallas_call(
        term_kernel,
        in_specs=[VMEM] * 2,
        out_specs=VMEM,
        out_shape=jax.ShapeDtypeStruct((NX * NZ, 16, LANES), F32),
        compiler_params=PARAMS,
        cost_estimate=cost(2**23, 2**20),
        name="term_part",
    )(recv, mean)


def spread_kernel(recv, send):
    total = recv[0, 0:8]
    for g in range(1, NX * NZ):
        total = total + recv[g, 0:8]
    for i in range(8 * NZ):
        send[i] = total


def spread(recv):
    return pl.pallas_call(
        spread_kernel,
        in_specs=[VMEM],
        out_specs=VMEM,
        out_shape=jax.ShapeDtypeStruct((8 * NZ, 8, LANES), F32),
        compiler_params=PARAMS,
        cost_estimate=cost(2**15, 2**19),
        name="spread",
    )(recv)


def inverse_factor(gram):
    row = lax.broadcasted_iota(jnp.int32, (32, 32), 0)
    lane = lax.broadcasted_iota(jnp.int32, (32, 32), 1)
    unit = jnp.where(lane == row, 1.0, 0.0).astype(F32)
    scale = jnp.zeros((32, 32), F32)
    for j in range(32):
        column = gram[:, j : j + 1]
        pivot = column[j : j + 1]
        scale = jnp.where(row == j, pivot, scale)
        share = jnp.where(row > j, column / pivot, 0.0)
        gram = gram - share * gram[j : j + 1]
        unit = unit - share * unit[j : j + 1]
    return unit / jnp.sqrt(scale)


def solve_kernel(recv, out):
    z = lax.axis_index("z")
    packed = recv[:, 8:16, :].reshape(NX * NZ * 8, LANES)
    low, high = packed[:, :64], packed[:, 64:]
    square = dot(low, low, ((0,), (0,))) + dot(high, high, ((0,), (0,)))
    inverse = inverse_factor(square[:32, :32] + square[32:, 32:])
    blank = jnp.zeros((32, 32), F32)
    wide = jnp.concatenate(
        [jnp.concatenate([inverse, blank], axis=1), jnp.concatenate([blank, inverse], axis=1)],
        axis=0,
    )
    mine = []
    for part in range(NX):
        block = recv[part * NZ + z, 8:16]
        mine += [block[:, :64], block[:, 64:]]
    out[:, :64] = dot(jnp.concatenate(mine, axis=0), wide, ((1,), (1,)))
    out[:, 64:] = wide


def solve(recv):
    return pl.pallas_call(
        solve_kernel,
        in_specs=[VMEM],
        out_specs=VMEM,
        out_shape=jax.ShapeDtypeStruct((64, LANES), F32),
        compiler_params=PARAMS,
        cost_estimate=cost(2**24, 2**19),
        name="solve",
    )(recv)


def solutions(mine, other):
    c = lax.axis_index("c")
    solved = [jnp.where(c == m, mine[...], other[...]) for m in range(2)]
    blank = jnp.zeros((32, 32), F32)
    inverse = jnp.concatenate(
        [
            jnp.concatenate([solved[0][:32, 64:96], blank], axis=1),
            jnp.concatenate([blank, solved[1][:32, 64:96]], axis=1),
        ],
        axis=0,
    )
    rows = [
        [solved[m][16 * x : 16 * x + 16, 32 * c : 32 * c + 32] for x, c in LOOP] for m in range(2)
    ]
    return inverse, rows


def approx_kernel(recv, mine, other, send, basis_out):
    z = lax.axis_index("z")
    inverse, rows = solutions(mine, other)
    columns = [
        jnp.concatenate([recv[DIAGONALS.index((a, part))] for part in range(NZ)], axis=0)
        for a in range(8)
    ]
    term = jnp.concatenate(columns, axis=1)
    turned = dot(inverse, term, ((1,), (0,)))
    own = turned[:, :LANES]
    for a in range(1, 8):
        own = jnp.where(z == a, turned[:, a * LANES : (a + 1) * LANES], own)
    basis_out[...] = own
    for m in range(2):
        result = dot(jnp.concatenate(rows[m], axis=0), turned[32 * m : 32 * (m + 1)], ((1,), (0,)))
        for i in range(NX * NC):
            send[i, m] = result[16 * i : 16 * i + 16]


def approx_part(recv, mine, other):
    return pl.pallas_call(
        approx_kernel,
        in_specs=[VMEM] * 3,
        out_specs=[VMEM] * 2,
        out_shape=[
            jax.ShapeDtypeStruct((NX * NC, 2, 16, 1024), F32),
            jax.ShapeDtypeStruct((64, LANES), F32),
        ],
        compiler_params=PARAMS,
        cost_estimate=cost(2**26, 2**20),
        name="approx_part",
    )(recv, mine, other)


def left_kernel(mine, other, out):
    x, c = lax.axis_index("x"), lax.axis_index("c")
    _, rows = solutions(mine, other)
    for m in range(2):
        left = rows[m][0]
        for i, (at, core) in enumerate(LOOP):
            left = jnp.where((x == at) & (c == core), rows[m][i], left)
        out[m] = left


def left_part(mine, other):
    return pl.pallas_call(
        left_kernel,
        in_specs=[VMEM] * 2,
        out_specs=VMEM,
        out_shape=jax.ShapeDtypeStruct((2, 16, 32), F32),
        compiler_params=PARAMS,
        cost_estimate=cost(2**22, 2**17),
        name="left_part",
    )(mine, other)


def subtract_kernel(merged, recv, out, result, sems):
    copies = []
    for x in range(NX):
        for m in range(2):
            for a in range(8):
                for c in range(NC):
                    at = pl.ds((x * 16 + 2 * a + c) * LANES, LANES)
                    approx = recv[LOOP.index((x, c)), m, :, a * LANES : (a + 1) * LANES]
                    result[m, :, at] = merged[2 * a + c, x, m] - approx
        copy = pltpu.make_async_copy(
            result.at[:, :, chunk(x)], out.at[0, :, :, chunk(x)], sems.at[x]
        )
        copy.start()
        copies.append(copy)
    for copy in copies:
        copy.wait()


def subtract(merged, recv):
    _, _, mats, rows, _ = merged.shape
    width = NX * 16 * LANES
    return pl.pallas_call(
        subtract_kernel,
        in_specs=[VMEM] * 2,
        out_specs=HBM,
        out_shape=jax.ShapeDtypeStruct((1, mats, rows, width), F32),
        scratch_shapes=[pltpu.VMEM((mats, rows, width), F32), pltpu.SemaphoreType.DMA((NX,))],
        compiler_params=PARAMS,
        cost_estimate=cost(2**19, 7 * 2**19),
        name="subtract",
    )(merged, recv)


def near_pairs():
    pairs = []
    for a in range(8):
        for dy, dz in ((0, -2), (1, -1), (2, 0), (-1, 1)):
            pairs.append(((a + dy) % 8 * NZ + a, a * NZ + (a + dz) % NZ))
    return pairs


def shards(grads, errors, basis):
    held = basis.transpose(1, 2, 0).reshape(64, LANES)
    held = lax.ppermute(held, ("y", "z"), near_pairs())
    held = relay(held)
    held = both(held, lax.ppermute(held, "z", [(z, (z + 4) % NZ) for z in range(NZ)]))
    merged = merge(grads, errors)
    recv = lax.all_to_all(merged, ("y", "c"), 0, 0)
    parts = [held] + [
        lax.ppermute(held, "x", [(i, (i + k) % NX) for i in range(NX)]) for k in range(1, NX)
    ]
    mean, send = factor_part(recv, arrange(parts))
    recv = lax.all_to_all(send, ("y", "c"), 0, 0)
    send = term_part(recv, mean)
    recv = lax.all_to_all(send, ("x", "z"), 0, 0)
    groups = [[y * NZ + z for y, z in DIAGONALS]]
    gathered = lax.all_to_all(spread(recv), ("y", "z"), 0, 0, axis_index_groups=groups)
    mine = solve(recv)
    other = lax.ppermute(mine, "c", [(0, 1), (1, 0)])
    left_factor, other = lax.optimization_barrier((left_part(mine, other), other))
    send, new_basis = approx_part(gathered, mine, other)
    groups = [[x * NC + c for x, c in LOOP]]
    recv = lax.all_to_all(send, ("x", "c"), 0, 0, axis_index_groups=groups)
    new_basis = new_basis.reshape(2, 32, LANES).transpose(2, 0, 1)
    return (subtract(merged, recv), left_factor, new_basis)


def solution(mesh):
    fine = Mesh(mesh.devices.reshape(8, NX, NZ, NC), ("y", "x", "z", "c"))
    fsdp = ("x", "z", "c")
    in_specs = (P("y", None, fsdp, None), P("y", None, fsdp, None), P(fsdp, None, None))
    out_specs = (P("y", None, fsdp, None), P(None, fsdp, None), P(fsdp, None, None))
    return jax.shard_map(shards, mesh=fine, in_specs=in_specs, out_specs=out_specs, check_vma=False)
```

```python
import jax
import jax.numpy as jnp
from jax import lax
from jax.experimental import pallas as pl
from jax.experimental.pallas import tpu as pltpu
from jax.sharding import Mesh, PartitionSpec as P

NX, NZ, NC = 4, 8, 2
LOOP = [(x, 0) for x in range(NX)] + [(x, 1) for x in reversed(range(NX))]
DIAGONALS = [((i + z) % 8, z) for i in range(8) for z in range(NZ)]
LANES = 128
HIGHEST = lax.Precision.HIGHEST
F32 = jnp.float32
VMEM = pl.BlockSpec(memory_space=pltpu.VMEM)
HBM = pl.BlockSpec(memory_space=pltpu.HBM)
PARAMS = pltpu.CompilerParams(vmem_limit_bytes=16 * 2**20)


def cost(flops, moved):
    return pl.CostEstimate(flops=flops, bytes_accessed=moved, transcendentals=0)


def dot(a, b, dims):
    return lax.dot_general(a, b, (dims, ((), ())), precision=HIGHEST, preferred_element_type=F32)


def chunk(x):
    return pl.ds(x * 16 * LANES, 16 * LANES)


def merge_kernel(grads, errors, out, grads_in, errors_in, blocks, sems):
    copies, results = [], []
    for h in range(2 * NX):
        at = pl.ds(h * 8 * LANES, 8 * LANES)
        for k, (source, target) in enumerate(((grads, grads_in), (errors, errors_in))):
            copy = pltpu.make_async_copy(source.at[0, :, :, at], target.at[:, :, at], sems.at[k, h])
            copy.start()
            copies.append(copy)
    for h in range(2 * NX):
        copies[2 * h].wait()
        copies[2 * h + 1].wait()
        x, first = h // 2, h % 2 * 8
        for m in range(2):
            for block in range(first, first + 8):
                at = pl.ds((x * 16 + block) * LANES, LANES)
                blocks[block, x, m] = grads_in[m, :, at].astype(F32) + errors_in[m, :, at]
        some = pl.ds(first, 8)
        copy = pltpu.make_async_copy(blocks.at[some, x], out.at[some, x], sems.at[2, h])
        copy.start()
        results.append(copy)
    for copy in results:
        copy.wait()


def merge(grads, errors):
    _, mats, rows, width = grads.shape
    return pl.pallas_call(
        merge_kernel,
        in_specs=[HBM] * 2,
        out_specs=HBM,
        out_shape=jax.ShapeDtypeStruct((16, NX, mats, rows, LANES), F32),
        scratch_shapes=[
            pltpu.VMEM((mats, rows, width), grads.dtype),
            pltpu.VMEM((mats, rows, width), errors.dtype),
            pltpu.VMEM((16, NX, mats, rows, LANES), F32),
            pltpu.SemaphoreType.DMA((3, 2 * NX)),
        ],
        cost_estimate=cost(2**19, 5 * 2**19),
        name="merge",
    )(grads, errors)


def relay_kernel(block, out):
    out[...] = block[...]


def relay(block):
    return pl.pallas_call(
        relay_kernel,
        in_specs=[VMEM],
        out_specs=VMEM,
        out_shape=jax.ShapeDtypeStruct(block.shape, F32),
        compiler_params=PARAMS,
        cost_estimate=cost(2**35, 2**16),
        name="relay",
    )(block)


def both_kernel(a, b, out):
    out[...] = a[...] + b[...]


def both(a, b):
    return pl.pallas_call(
        both_kernel,
        in_specs=[VMEM] * 2,
        out_specs=VMEM,
        out_shape=jax.ShapeDtypeStruct(a.shape, F32),
        compiler_params=PARAMS,
        cost_estimate=cost(2**13, 2**17),
        name="both",
    )(a, b)


def arrange_kernel(b0, b1, b2, b3, out):
    x = lax.axis_index("x")
    for part in range(NX):
        back = lax.rem(x - part + NX, NX)
        chosen = b0[...]
        for k, block in ((1, b1), (2, b2), (3, b3)):
            chosen = jnp.where(back == k, block[...], chosen)
        out[:, part * LANES : (part + 1) * LANES] = chosen


def arrange(shards):
    return pl.pallas_call(
        arrange_kernel,
        in_specs=[VMEM] * 4,
        out_specs=VMEM,
        out_shape=jax.ShapeDtypeStruct((64, NX * LANES), F32),
        compiler_params=PARAMS,
        cost_estimate=cost(2**20, 2**18),
        name="arrange",
    )(*shards)


def factor_kernel(recv, weights, mean_out, send):
    columns = []
    for part in range(NX):
        blocks = []
        for m in range(2):
            for c in range(NC):
                total = recv[c, part, m]
                for a in range(1, 8):
                    total = total + recv[2 * a + c, part, m]
                blocks.append(total)
        columns.append(jnp.concatenate(blocks, axis=0) * 0.125)
    mean = jnp.concatenate(columns, axis=1)
    mean_out[...] = mean
    partial = dot(mean, weights[...], ((1,), (1,)))
    piece = jnp.concatenate(
        [
            partial[16 * (2 * m + c) : 16 * (2 * m + c + 1), 32 * m : 32 * (m + 1)]
            for m in range(2)
            for c in range(NC)
        ],
        axis=1,
    )
    for i in range(16):
        send[i] = piece


def factor_part(recv, weights):
    return pl.pallas_call(
        factor_kernel,
        in_specs=[VMEM] * 2,
        out_specs=[VMEM] * 2,
        out_shape=[
            jax.ShapeDtypeStruct((64, 512), F32),
            jax.ShapeDtypeStruct((16, 16, LANES), F32),
        ],
        compiler_params=PARAMS,
        cost_estimate=cost(2**22, 2**20 + 2**19),
        name="factor_part",
    )(recv, weights)


def term_kernel(recv, mean, send):
    factor = recv[0]
    for i in range(1, 16):
        factor = factor + recv[i]
    blank = jnp.zeros((16, 32), F32)
    rows = []
    for m in range(2):
        for c in range(NC):
            piece = factor[:, 32 * (2 * m + c) : 32 * (2 * m + c + 1)]
            rows.append(jnp.concatenate([piece, blank] if m == 0 else [blank, piece], axis=1))
    blocked = jnp.concatenate(rows, axis=0)
    half = jnp.where(lax.axis_index("c") == 0, factor[:, :64], factor[:, 64:])
    half = jnp.concatenate([half[:8], half[8:]], axis=1)
    term = dot(blocked, mean[...], ((0,), (0,)))
    for x in range(NX):
        for z in range(NZ):
            send[x * NZ + z, 0:8] = term[8 * z : 8 * z + 8, x * LANES : (x + 1) * LANES]
            send[x * NZ + z, 8:16] = half


def term_part(recv, mean):
    return pl.pallas_call(
        term_kernel,
        in_specs=[VMEM] * 2,
        out_specs=VMEM,
        out_shape=jax.ShapeDtypeStruct((NX * NZ, 16, LANES), F32),
        compiler_params=PARAMS,
        cost_estimate=cost(2**23, 2**20),
        name="term_part",
    )(recv, mean)


def spread_kernel(recv, send):
    total = recv[0, 0:8]
    for g in range(1, NX * NZ):
        total = total + recv[g, 0:8]
    for i in range(8 * NZ):
        send[i] = total


def spread(recv):
    return pl.pallas_call(
        spread_kernel,
        in_specs=[VMEM],
        out_specs=VMEM,
        out_shape=jax.ShapeDtypeStruct((8 * NZ, 8, LANES), F32),
        compiler_params=PARAMS,
        cost_estimate=cost(2**15, 2**19),
        name="spread",
    )(recv)


def inverse_factor(gram):
    row = lax.broadcasted_iota(jnp.int32, (32, 32), 0)
    lane = lax.broadcasted_iota(jnp.int32, (32, 32), 1)
    unit = jnp.where(lane == row, 1.0, 0.0).astype(F32)
    scale = jnp.zeros((32, 32), F32)
    for j in range(32):
        column = gram[:, j : j + 1]
        pivot = column[j : j + 1]
        scale = jnp.where(row == j, pivot, scale)
        share = jnp.where(row > j, column / pivot, 0.0)
        gram = gram - share * gram[j : j + 1]
        unit = unit - share * unit[j : j + 1]
    return unit / jnp.sqrt(scale)


def solve_kernel(recv, out):
    z = lax.axis_index("z")
    packed = recv[:, 8:16, :].reshape(NX * NZ * 8, LANES)
    low, high = packed[:, :64], packed[:, 64:]
    square = dot(low, low, ((0,), (0,))) + dot(high, high, ((0,), (0,)))
    inverse = inverse_factor(square[:32, :32] + square[32:, 32:])
    blank = jnp.zeros((32, 32), F32)
    wide = jnp.concatenate(
        [jnp.concatenate([inverse, blank], axis=1), jnp.concatenate([blank, inverse], axis=1)],
        axis=0,
    )
    mine = []
    for part in range(NX):
        block = recv[part * NZ + z, 8:16]
        mine += [block[:, :64], block[:, 64:]]
    out[:, :64] = dot(jnp.concatenate(mine, axis=0), wide, ((1,), (1,)))
    out[:, 64:] = wide


def solve(recv):
    return pl.pallas_call(
        solve_kernel,
        in_specs=[VMEM],
        out_specs=VMEM,
        out_shape=jax.ShapeDtypeStruct((64, LANES), F32),
        compiler_params=PARAMS,
        cost_estimate=cost(2**24, 2**19),
        name="solve",
    )(recv)


def solutions(mine, other):
    c = lax.axis_index("c")
    solved = [jnp.where(c == m, mine[...], other[...]) for m in range(2)]
    blank = jnp.zeros((32, 32), F32)
    inverse = jnp.concatenate(
        [
            jnp.concatenate([solved[0][:32, 64:96], blank], axis=1),
            jnp.concatenate([blank, solved[1][:32, 64:96]], axis=1),
        ],
        axis=0,
    )
    rows = [
        [solved[m][16 * x : 16 * x + 16, 32 * c : 32 * c + 32] for x, c in LOOP] for m in range(2)
    ]
    return inverse, rows


def approx_kernel(recv, mine, other, send, basis_out):
    z = lax.axis_index("z")
    inverse, rows = solutions(mine, other)
    columns = [
        jnp.concatenate([recv[DIAGONALS.index((a, part))] for part in range(NZ)], axis=0)
        for a in range(8)
    ]
    term = jnp.concatenate(columns, axis=1)
    turned = dot(inverse, term, ((1,), (0,)))
    own = turned[:, :LANES]
    for a in range(1, 8):
        own = jnp.where(z == a, turned[:, a * LANES : (a + 1) * LANES], own)
    basis_out[...] = own
    for m in range(2):
        result = dot(jnp.concatenate(rows[m], axis=0), turned[32 * m : 32 * (m + 1)], ((1,), (0,)))
        for i in range(NX * NC):
            send[i, m] = result[16 * i : 16 * i + 16]


def approx_part(recv, mine, other):
    return pl.pallas_call(
        approx_kernel,
        in_specs=[VMEM] * 3,
        out_specs=[VMEM] * 2,
        out_shape=[
            jax.ShapeDtypeStruct((NX * NC, 2, 16, 1024), F32),
            jax.ShapeDtypeStruct((64, LANES), F32),
        ],
        compiler_params=PARAMS,
        cost_estimate=cost(2**26, 2**20),
        name="approx_part",
    )(recv, mine, other)


def left_kernel(mine, other, out):
    x, c = lax.axis_index("x"), lax.axis_index("c")
    _, rows = solutions(mine, other)
    for m in range(2):
        left = rows[m][0]
        for i, (at, core) in enumerate(LOOP):
            left = jnp.where((x == at) & (c == core), rows[m][i], left)
        out[m] = left


def left_part(mine, other):
    return pl.pallas_call(
        left_kernel,
        in_specs=[VMEM] * 2,
        out_specs=VMEM,
        out_shape=jax.ShapeDtypeStruct((2, 16, 32), F32),
        compiler_params=PARAMS,
        cost_estimate=cost(2**22, 2**17),
        name="left_part",
    )(mine, other)


def subtract_kernel(merged, recv, out, result, sems):
    copies = []
    for x in range(NX):
        for m in range(2):
            for a in range(8):
                for c in range(NC):
                    at = pl.ds((x * 16 + 2 * a + c) * LANES, LANES)
                    approx = recv[LOOP.index((x, c)), m, :, a * LANES : (a + 1) * LANES]
                    result[m, :, at] = merged[2 * a + c, x, m] - approx
        copy = pltpu.make_async_copy(
            result.at[:, :, chunk(x)], out.at[0, :, :, chunk(x)], sems.at[x]
        )
        copy.start()
        copies.append(copy)
    for copy in copies:
        copy.wait()


def subtract(merged, recv):
    _, _, mats, rows, _ = merged.shape
    width = NX * 16 * LANES
    return pl.pallas_call(
        subtract_kernel,
        in_specs=[VMEM] * 2,
        out_specs=HBM,
        out_shape=jax.ShapeDtypeStruct((1, mats, rows, width), F32),
        scratch_shapes=[pltpu.VMEM((mats, rows, width), F32), pltpu.SemaphoreType.DMA((NX,))],
        compiler_params=PARAMS,
        cost_estimate=cost(2**19, 7 * 2**19),
        name="subtract",
    )(merged, recv)


def near_pairs():
    pairs = []
    for a in range(8):
        for dy, dz in ((0, -2), (1, -1), (2, 0), (-1, 1)):
            pairs.append(((a + dy) % 8 * NZ + a, a * NZ + (a + dz) % NZ))
    return pairs


def shards(grads, errors, basis):
    held = basis.transpose(1, 2, 0).reshape(64, LANES)
    held = lax.ppermute(held, ("y", "z"), near_pairs())
    held = relay(held)
    held = both(held, lax.ppermute(held, "z", [(z, (z + 4) % NZ) for z in range(NZ)]))
    merged = merge(grads, errors)
    recv = lax.all_to_all(merged, ("y", "c"), 0, 0)
    moved = {
        k: lax.ppermute(held, "x", [(i, (i + k) % NX) for i in range(NX)]) for k in (2, 1, 3)
    }
    parts = [held] + [moved[k] for k in range(1, NX)]
    mean, send = factor_part(recv, arrange(parts))
    recv = lax.all_to_all(send, ("y", "c"), 0, 0)
    send = term_part(recv, mean)
    recv = lax.all_to_all(send, ("x", "z"), 0, 0)
    groups = [[y * NZ + z for y, z in DIAGONALS]]
    gathered = lax.all_to_all(spread(recv), ("y", "z"), 0, 0, axis_index_groups=groups)
    mine = solve(recv)
    other = lax.ppermute(mine, "c", [(0, 1), (1, 0)])
    left_factor, other = lax.optimization_barrier((left_part(mine, other), other))
    send, new_basis = approx_part(gathered, mine, other)
    groups = [[x * NC + c for x, c in LOOP]]
    recv = lax.all_to_all(send, ("x", "c"), 0, 0, axis_index_groups=groups)
    new_basis = new_basis.reshape(2, 32, LANES).transpose(2, 0, 1)
    return (subtract(merged, recv), left_factor, new_basis)


def solution(mesh):
    fine = Mesh(mesh.devices.reshape(8, NX, NZ, NC), ("y", "x", "z", "c"))
    fsdp = ("x", "z", "c")
    in_specs = (P("y", None, fsdp, None), P("y", None, fsdp, None), P(fsdp, None, None))
    out_specs = (P("y", None, fsdp, None), P(None, fsdp, None), P(fsdp, None, None))
    return jax.shard_map(shards, mesh=fine, in_specs=in_specs, out_specs=out_specs, check_vma=False)
```
